256 devices in a mesh: dp: 16 (over y, z_hi), tp: 16 (over x, z_lo, core).
Axes of the slice: x: 4, y: 4, z: 8 (z_hi: 4, z_lo: 2; z = z_hi * 2 + z_lo), core: 2. Of those that a mesh axis runs over, the one named last changes fastest.
Arguments:
- input_rows: bfloat16 [16, 2048, 4096], P('dp', 'tp'), may hold values from -6 to 6
- queries: bfloat16 [16, 2048, 4096], P('dp', None, 'tp')
- key_values: bfloat16 [16, 2048, 1024], P('dp')
- out_grad: bfloat16 [16, 2048, 4096], P('dp', None, 'tp'), may hold values from -6 to 6
- item_logratio: float32 [16, 4], P('dp'), may hold values from -40 to 40
- pair_ids: int32 [16, 4], P('dp'), may hold values from 0 to 1, as said below
- tile_item: int32 [16, 16], P('dp'), may hold values from 0 to 3, as said below
- tile_image: int32 [16, 16], P('dp'), may hold values from 0 to 16, as said below
Outputs:
- grad_query: bfloat16 [16, 2048, 4096], P('dp', None, 'tp')
- grad_kv_weight: float32 [4096, 1024], P('dp', 'tp')
The draws below stay inside these ranges and needn't reach their ends.
Inputs may be any that keep to these rules, and one draw needn't show every extreme that they name: Each sequence's tile_item never falls, starts at 0 and ends at 3; a response may have no tiles. `tile_image`: image tiles carry 1 plus the index of the first tile of their image; an image is a maximal run of image tiles inside one response; the last tile of a sequence is an image tile and the one before it is text. `pair_ids`: within a sequence each pair id appears for exactly two responses; the earlier of the two is the chosen response.
All inputs are finite; a program needn't handle non-finite values.
Results may differ from the reference program's by a relative error of at most 0.0065.
Values may be sent and summed in bfloat16 or wider, within the bound.
A program may use at most 128 MiB of HBM per device.

```python
import math
import jax
import jax.numpy as jnp
from jax import lax

D = 4096
H = 32
KVH = 4
HD = 128
TILE = 128
ITEMS = 4
L = 2048
NT = 16
SEQS = 16


def layout(key):
    key_cut, key_flag = jax.random.split(jax.random.fold_in(key, 11))
    bounds = jax.random.randint(key_cut, (SEQS, ITEMS - 1), 1, NT).astype(jnp.int32)
    tile_index = jnp.arange(NT, dtype=jnp.int32)[None, :]
    items = jnp.sum((bounds[:, None, :] <= tile_index[:, :, None]).astype(jnp.int32), axis=2).astype(jnp.int32)
    starts = jnp.concatenate([jnp.zeros((SEQS, 1), jnp.int32), items[:, 1:] - items[:, :-1]], axis=1)
    starts = jnp.minimum(starts, 1).astype(jnp.int32)
    flags = jax.random.randint(key_flag, (SEQS, NT), 0, 2).astype(jnp.int32)
    flags = jnp.where(tile_index == NT - 1, 1, jnp.where(tile_index == NT - 2, 0, flags)).astype(jnp.int32)
    before = jnp.concatenate([jnp.zeros((SEQS, 1), jnp.int32), flags[:, :-1]], axis=1)
    begins = flags * jnp.maximum(1 - before, starts)
    begin_label = jnp.where(begins > 0, tile_index + 1, 0).astype(jnp.int32)
    images = (lax.cummax(begin_label, axis=1) * flags).astype(jnp.int32)
    return (items, images)


def draw_queries(key, part):
    key = jax.random.fold_in(key, 1)
    drawn = jax.random.normal(key, (SEQS, L, H, HD), jnp.float32)
    return drawn.reshape(SEQS, L, H * HD).astype(jnp.bfloat16)


def draw_key_values(key, part):
    key = jax.random.fold_in(key, 2)
    drawn = jax.random.normal(key, (SEQS, L, KVH, 2, HD), jnp.float32)
    return drawn.reshape(SEQS, L, 2 * KVH * HD).astype(jnp.bfloat16)


def draw_pair_ids(key, part):
    key = jax.random.fold_in(key, 5)
    scores = jax.random.randint(key, (SEQS, ITEMS), 0, 1 << 20) * ITEMS + jnp.arange(ITEMS, dtype=jnp.int32)[None, :]
    ranks = jnp.argsort(jnp.argsort(scores, axis=1), axis=1)
    return (ranks // 2).astype(jnp.int32)


def draw_tile_item(key, part):
    items, images = layout(key)
    return items


def draw_tile_image(key, part):
    items, images = layout(key)
    return images


def strengthened(values, stream_key, source, target, parts, factor):
    owner, partner = [(jnp.arange(values.shape[dim]) // (values.shape[dim] // parts)).reshape([-1 if axis == dim else 1 for axis in range(values.ndim)]) for dim in (source, target)]
    chosen = jax.random.permutation(stream_key, parts)[partner]
    strong = (owner == chosen) | (owner == (partner + parts // 2) % parts)
    return jnp.where(strong, factor * values, values)


def block_scale(rng, dims, cuts, smallest, largest):
    def one(axis_at, parts):
        draws = jax.random.uniform(jax.random.fold_in(jax.random.fold_in(rng, 6), axis_at), (parts,), jnp.float32, smallest / len(cuts), largest / len(cuts))
        return jnp.repeat(jnp.exp(draws), dims[axis_at] // parts).reshape((-1,) + (1,) * (len(dims) - axis_at - 1))

    loudness = one(*cuts[0])
    for cut in cuts[1:]:
        loudness = loudness * one(*cut)
    return loudness


def bell_draw(rng, dims, width, most, cuts=(), held_as=jnp.bfloat16):
    result = width * jax.random.normal(rng, dims, jnp.float32)
    if cuts:
        result = result * block_scale(rng, dims, cuts, -0.22, 0.18)
    return jnp.clip(result, -most, most).astype(held_as)


def bell_draw_with(own_key, shape, scale, most, pieces, heavy, kind=jnp.bfloat16):
    values = scale * jax.random.normal(own_key, shape, jnp.float32)
    if pieces:
        values = values * block_scale(own_key, shape, pieces, -0.22, 0.18)
    return jnp.clip(strengthened(values, jax.random.fold_in(own_key, 3), *heavy), -most, most).astype(kind)


def setup_inputs(seed: int = 0) -> dict:
    seeds = jax.random.split(jax.random.key(seed), 9)
    return {
        "input_rows": bell_draw_with(seeds[0], (SEQS, L, D), 1.0, 6.0, ((0, 16), (1, 16)), (0, 2, 16, 2.0)),
        "queries": draw_queries(jax.random.fold_in(seeds[8], 71), 0),
        "key_values": draw_key_values(jax.random.fold_in(seeds[8], 71), 0),
        "out_grad": bell_draw(seeds[3], (SEQS, L, H * HD), 1.0, 6.0, ((0, 16), (2, 16))),
        "item_logratio": bell_draw(seeds[4], (SEQS, ITEMS), 8.0, 40.0, ((0, 16),), jnp.float32),
        "pair_ids": draw_pair_ids(jax.random.fold_in(seeds[8], 71), 0),
        "tile_item": draw_tile_item(jax.random.fold_in(seeds[8], 71), 0),
        "tile_image": draw_tile_image(jax.random.fold_in(seeds[8], 71), 0),
    }


BETA = 0.1
MASKED = -1e+30

def item_weights(ratios, pair_list):
    item_index = jnp.arange(ratios.shape[0], dtype=jnp.int32)
    paired = (pair_list[:, None] == pair_list[None, :]) & (item_index[:, None] != item_index[None, :])
    partner_ratio = lax.optimization_barrier(jnp.sum(jnp.where(paired, ratios[None, :], 0.0), axis=1))
    partner_index = lax.optimization_barrier(jnp.sum(jnp.where(paired, item_index[None, :], 0), axis=1))
    polarity = jnp.where(item_index < partner_index, -1.0, 1.0).astype(ratios.dtype)
    margin = BETA * polarity * (partner_ratio - ratios)
    return polarity * jax.nn.sigmoid(-margin)

def token_weights(weights_item, items_tok):
    choices_row = jnp.arange(weights_item.shape[0], dtype=jnp.int32)
    lookup = jnp.where(items_tok[:, None] == choices_row[None, :], weights_item[None, :], 0.0)
    return lax.optimization_barrier(jnp.sum(lookup, axis=1))

def attend_mask(rows_item, rows_image, rows_pos, cols_item, cols_image, cols_pos):
    same_item = rows_item[:, None] == cols_item[None, :]
    causal = cols_pos[None, :] <= rows_pos[:, None]
    same_image = (rows_image[:, None] == cols_image[None, :]) & (rows_image[:, None] > 0)
    return same_item & (causal | same_image)

def one_sequence(x_rows, queries, key_values, out_grad, ratios, pair_list, items_tile, images_tile):
    length = queries.shape[0]
    inv_root = 1.0 / math.sqrt(HD)
    items_tok = jnp.repeat(items_tile, TILE)
    images_tok = jnp.repeat(images_tile, TILE)
    positions = jnp.arange(length, dtype=jnp.int32)
    allowed = attend_mask(items_tok, images_tok, positions, items_tok, images_tok, positions)
    factors = token_weights(item_weights(ratios, pair_list), items_tok)
    weighted = (out_grad.astype(jnp.float32) * factors[:, None]).astype(jnp.bfloat16)
    query_heads = queries.reshape(length, H, HD)
    weighted_heads = weighted.reshape(length, H, HD)
    kv_heads = key_values.reshape(length, KVH, 2, HD)

    def per_head(head_index):
        kv_index = head_index // (H // KVH)
        query_rows = lax.dynamic_index_in_dim(query_heads, head_index, 1, keepdims=False)
        weighted_rows = lax.dynamic_index_in_dim(weighted_heads, head_index, 1, keepdims=False)
        kv_rows = lax.dynamic_index_in_dim(kv_heads, kv_index, 1, keepdims=False)
        key_rows = kv_rows[:, 0]
        value_rows = kv_rows[:, 1]
        scores = jnp.dot(query_rows, key_rows.T, preferred_element_type=jnp.float32) * inv_root
        scores = jnp.where(allowed, scores, MASKED)
        row_max = lax.optimization_barrier(jnp.max(scores, axis=1, keepdims=True))
        unnorm = jnp.where(allowed, jnp.exp(scores - row_max), 0.0)
        attend = unnorm / lax.optimization_barrier(jnp.sum(unnorm, axis=1, keepdims=True))
        attend_low = attend.astype(jnp.bfloat16)
        dprob = jnp.dot(weighted_rows, value_rows.T, preferred_element_type=jnp.float32)
        rowdot = lax.optimization_barrier(jnp.sum(attend * dprob, axis=1, keepdims=True))
        dscore = (attend * (dprob - rowdot)).astype(jnp.bfloat16)
        grad_rows = (jnp.dot(dscore, key_rows, preferred_element_type=jnp.float32) * inv_root).astype(jnp.bfloat16)
        key_grad = jnp.dot(dscore.T, query_rows, preferred_element_type=jnp.float32) * inv_root
        value_grad = jnp.dot(attend_low.T, weighted_rows, preferred_element_type=jnp.float32)
        return (grad_rows, key_grad, value_grad)
    grad_heads, key_grads, value_grads = lax.map(per_head, jnp.arange(H, dtype=jnp.int32))
    key_sum = key_grads.reshape(KVH, H // KVH, length, HD).sum(axis=1)
    value_sum = value_grads.reshape(KVH, H // KVH, length, HD).sum(axis=1)
    grads_kv = jnp.stack([key_sum, value_sum], axis=2)
    grads_kv = jnp.transpose(grads_kv, (1, 0, 2, 3)).reshape(length, KVH * 2 * HD)
    weight_grad = lax.dot_general(x_rows.astype(jnp.float32), grads_kv, (((0,), (0,)), ((), ())), precision=lax.Precision.HIGHEST)
    grad_query = jnp.transpose(grad_heads, (1, 0, 2)).reshape(length, H * HD)
    return (grad_query, weight_grad)

def reference(input_rows, queries, key_values, out_grad, item_logratio, pair_ids, tile_item, tile_image):

    def advance(running, packed):
        grad_query, weight_grad = one_sequence(*packed)
        return (running + weight_grad, grad_query)
    initial = jnp.zeros((D, 2 * KVH * HD), jnp.float32)
    running, grad_query = lax.scan(advance, initial, (input_rows, queries, key_values, out_grad, item_logratio, pair_ids, tile_item, tile_image))
    return (grad_query, running)
```

```python
import functools, math
import jax, jax.numpy as jnp
from jax import lax
from jax.experimental import pallas as pl
from jax.experimental.pallas import tpu as pltpu

from jax.sharding import PartitionSpec as P

KVH = 4; HD = 128; TILE = 128; BETA = 0.1
MASKED = -1e30
LOG2E = 1.4426950408889634

def attention_kernel(ratio, pair, item, image, q_ref, og_ref, kv_hbm, dq_ref, kvt_ref,
                     kv, s_scr, dp_scr, acc, lo_s, hi_s, z_s, kv_sem):
    group = lax.axis_size("tp") // KVH
    g = lax.axis_index("tp") // group
    load = pltpu.make_async_copy(kv_hbm.at[0, :, pl.ds(pl.multiple_of(g * 2 * HD, 2 * HD), 2 * HD)], kv, kv_sem)
    load.start()
    nt = 16
    items = ratio.shape[1]
    inv_root = 1.0 / math.sqrt(HD)
    c2 = inv_root * LOG2E
    acc[...] = jnp.zeros_like(acc)
    lo_s[0] = 0
    for i in range(1, nt):
        lo_s[i] = jnp.where(item[0, i] == item[0, i - 1], lo_s[i - 1], i)
    hi_s[nt - 1] = nt - 1
    for i in reversed(range(nt - 1)):
        same = (image[0, i] > 0) & (image[0, i] == image[0, i + 1]) & (item[0, i] == item[0, i + 1])
        hi_s[i] = jnp.where(same, hi_s[i + 1], i)
    for a in range(items):
        other = jnp.float32(0.0)
        p = jnp.float32(1.0)
        for b in range(items):
            if b != a:
                same = pair[0, a] == pair[0, b]
                other = other + jnp.where(same, ratio[0, b], 0.0)
                if a < b:
                    p = jnp.where(same, -1.0, p)
        z_s[a] = BETA * p * (other - ratio[0, a])
        z_s[items + a] = p
    load.wait()

    def row_tile(I, carry):
        lo = lo_s[I]
        hi = hi_s[I]
        img = image[0, I]
        it = item[0, I]
        r0 = pl.multiple_of(I * TILE, TILE)
        qi = q_ref[0, pl.ds(r0, TILE), :]
        q2 = jnp.concatenate([qi[:, :HD], qi[:, HD:]], axis=0)
        coef = z_s[items + it] / (1.0 + jnp.exp(jnp.full((8, HD), z_s[it], jnp.float32)))
        coef = jnp.concatenate([coef[:1], coef[:1]], axis=1)
        wi = (og_ref[0, pl.ds(r0, TILE), :].astype(jnp.float32) * coef).astype(jnp.bfloat16)
        w2 = jnp.concatenate([wi[:, :HD], wi[:, HD:]], axis=0)
        q2t = q2.T
        w2t = w2.T
        tiles = hi - lo + 1
        chunks = (tiles + 1) // 2

        def body(n):
            st_t = jnp.minimum(lo, nt - 2 * n)
            st = pl.multiple_of(st_t * TILE, TILE)
            W = 2 * TILE
            row = lax.broadcasted_iota(jnp.int32, (TILE, 1), 0)
            row = jnp.concatenate([row, row], axis=0)
            first = lo * TILE - st
            last = jnp.where(img > 0, jnp.full((2 * TILE, 1), (hi + 1) * TILE - 1 - st), r0 - st + row)
            m = None
            for ch in range(n):
                kc = kv[pl.ds(st + ch * W, W), :HD]
                vc = kv[pl.ds(st + ch * W, W), HD:]
                s = lax.dot_general(q2, kc, (((1,), (1,)), ((), ())), preferred_element_type=jnp.float32)
                if ch == 0 or ch == n - 1:
                    col = lax.broadcasted_iota(jnp.int32, (1, W), 1) + ch * W
                    ok = col <= last
                    if ch == 0 or n == 1:
                        ok = ok & (col >= first)
                    s = jnp.where(ok, s, MASKED)
                s_scr[:, ch * W:(ch + 1) * W] = s
                mm = jnp.maximum(s[:, :HD], s[:, HD:])
                m = mm if m is None else jnp.maximum(m, mm)
                dp_scr[:, ch * W:(ch + 1) * W] = lax.dot_general(w2, vc, (((1,), (1,)), ((), ())), preferred_element_type=jnp.float32)
            mr = jnp.max(m, axis=1, keepdims=True) * c2
            l = None
            for ch in range(n):
                p = jnp.exp2(s_scr[:, ch * W:(ch + 1) * W] * c2 - mr)
                s_scr[:, ch * W:(ch + 1) * W] = p
                pd = p * dp_scr[:, ch * W:(ch + 1) * W]
                ll = p[:, :HD] + p[:, HD:]
                rr = pd[:, :HD] + pd[:, HD:]
                l = ll if l is None else l + ll
                r = rr if ch == 0 else r + rr
            inv = 1.0 / jnp.sum(l, axis=1, keepdims=True)
            rd = jnp.sum(r, axis=1, keepdims=True) * inv
            dq = None
            for ch in range(n):
                kc = kv[pl.ds(st + ch * W, W), :HD]
                at = s_scr[:, ch * W:(ch + 1) * W] * inv
                ds = (at * (dp_scr[:, ch * W:(ch + 1) * W] - rd)).astype(jnp.bfloat16)
                at = at.astype(jnp.bfloat16)
                d = jnp.dot(ds, kc, preferred_element_type=jnp.float32)
                dq = d if dq is None else dq + d
                cols = pl.ds(st + ch * W, W)
                acc[:HD, cols] += jnp.dot(q2t, ds, preferred_element_type=jnp.float32)
                acc[HD:, cols] += jnp.dot(w2t, at, preferred_element_type=jnp.float32)
            dq = (dq * inv_root).astype(jnp.bfloat16)
            dq_ref[0, pl.ds(r0, TILE), :HD] = dq[:TILE]
            dq_ref[0, pl.ds(r0, TILE), HD:] = dq[TILE:]

        for n in range(1, nt // 2 + 1):
            @pl.when(chunks == n)
            def _():
                body(n)
        return carry

    lax.fori_loop(0, nt, row_tile, 0)
    kvt_ref[:HD] = (acc[:HD] * inv_root).astype(jnp.bfloat16)
    kvt_ref[HD:] = acc[HD:].astype(jnp.bfloat16)


def attention(queries, out_grad, key_values, ratio, pair, item, image):
    L = queries.shape[1]
    nt = L // TILE
    smem = pl.BlockSpec(memory_space=pltpu.SMEM)
    vmem = pl.BlockSpec(memory_space=pltpu.VMEM)
    return pl.pallas_call(
        attention_kernel,
        out_shape=[jax.ShapeDtypeStruct(queries.shape, jnp.bfloat16),
                   jax.ShapeDtypeStruct((2 * HD, L), jnp.bfloat16)],
        in_specs=[smem] * 4 + [vmem, vmem, pl.BlockSpec(memory_space=pl.ANY)],
        out_specs=[vmem, vmem],
        scratch_shapes=[
            pltpu.VMEM((L, 2 * HD), jnp.bfloat16),
            pltpu.VMEM((2 * TILE, L), jnp.float32),
            pltpu.VMEM((2 * TILE, L), jnp.float32),
            pltpu.VMEM((2 * HD, L), jnp.float32),
            pltpu.SMEM((nt,), jnp.int32),
            pltpu.SMEM((nt,), jnp.int32),
            pltpu.SMEM((2 * ratio.shape[1],), jnp.float32),
            pltpu.SemaphoreType.DMA,
        ],
        compiler_params=pltpu.CompilerParams(vmem_limit_bytes=48 << 20),
        cost_estimate=pl.CostEstimate(flops=10 * 10**9, bytes_accessed=8 << 20, transcendentals=0),
        name="attention",
    )(ratio, pair, item, image, queries, out_grad, key_values)


def local(input_rows, queries, key_values, out_grad, item_logratio, pair_ids, tile_item, tile_image):
    tp = lax.axis_size("tp")
    t = lax.axis_index("tp")
    xc = lax.all_to_all(input_rows[0], "tp", 1, 0, tiled=True)
    dq, part = attention(queries, out_grad, key_values, item_logratio, pair_ids, tile_item, tile_image)
    for bit in (1, 0):
        half = part.shape[0] // 2
        mine = t // 2**bit % 2
        kept = lax.dynamic_slice_in_dim(part, mine * half, half, 0)
        sent = lax.dynamic_slice_in_dim(part, (1 - mine) * half, half, 0)
        got = lax.ppermute(sent, "tp", [(i, i ^ 1 << bit) for i in range(tp)])
        part = (kept.astype(jnp.float32) + got.astype(jnp.float32)).astype(jnp.bfloat16)
    whole = lax.all_gather(part, "tp", axis=0, tiled=True)
    wt = jnp.dot(whole, xc, preferred_element_type=jnp.float32)
    wt = lax.psum_scatter(wt, "dp", scatter_dimension=0, tiled=True)
    wt = lax.ppermute(wt, ("dp", "tp"), [(a * tp + b, b * tp + a) for a in range(tp) for b in range(tp)])
    return dq, wt.T


def solution(mesh):
    in_specs = (P("dp", "tp", None), P("dp", None, "tp"), P("dp", None, None), P("dp", None, "tp"),
                P("dp", None), P("dp", None), P("dp", None), P("dp", None))
    out_specs = (P("dp", None, "tp"), P("dp", "tp"))
    return jax.shard_map(local, mesh=mesh, in_specs=in_specs, out_specs=out_specs, check_vma=False)
```

```python
import functools, math
import jax, jax.numpy as jnp
from jax import lax
from jax.experimental import pallas as pl
from jax.experimental.pallas import tpu as pltpu

from jax.sharding import PartitionSpec as P

KVH = 4; HD = 128; TILE = 128; BETA = 0.1
MASKED = -1e30
LOG2E = 1.4426950408889634

def attention_kernel(ratio, pair, item, image, q_ref, og_ref, kv_hbm, dq_ref, kvt_ref,
                     kv, s_scr, dp_scr, acc, lo_s, hi_s, z_s, kv_sem):
    group = lax.axis_size("tp") // KVH
    g = lax.axis_index("tp") // group
    load = pltpu.make_async_copy(kv_hbm.at[0, :, pl.ds(pl.multiple_of(g * 2 * HD, 2 * HD), 2 * HD)], kv, kv_sem)
    load.start()
    nt = 16
    items = ratio.shape[1]
    inv_root = 1.0 / math.sqrt(HD)
    c2 = inv_root * LOG2E
    acc[...] = jnp.zeros_like(acc)
    lo_s[0] = 0
    for i in range(1, nt):
        lo_s[i] = jnp.where(item[0, i] == item[0, i - 1], lo_s[i - 1], i)
    hi_s[nt - 1] = nt - 1
    for i in reversed(range(nt - 1)):
        same = (image[0, i] > 0) & (image[0, i] == image[0, i + 1]) & (item[0, i] == item[0, i + 1])
        hi_s[i] = jnp.where(same, hi_s[i + 1], i)
    for a in range(items):
        other = jnp.float32(0.0)
        p = jnp.float32(1.0)
        for b in range(items):
            if b != a:
                same = pair[0, a] == pair[0, b]
                other = other + jnp.where(same, ratio[0, b], 0.0)
                if a < b:
                    p = jnp.where(same, -1.0, p)
        z_s[a] = BETA * p * (other - ratio[0, a])
        z_s[items + a] = p
    load.wait()

    def row_tile(I, carry):
        lo = lo_s[I]
        hi = hi_s[I]
        img = image[0, I]
        it = item[0, I]
        r0 = pl.multiple_of(I * TILE, TILE)
        qi = q_ref[0, pl.ds(r0, TILE), :]
        q2 = jnp.concatenate([qi[:, :HD], qi[:, HD:]], axis=0)
        coef = z_s[items + it] / (1.0 + jnp.exp(jnp.full((8, HD), z_s[it], jnp.float32)))
        coef = jnp.concatenate([coef[:1], coef[:1]], axis=1)
        wi = (og_ref[0, pl.ds(r0, TILE), :].astype(jnp.float32) * coef).astype(jnp.bfloat16)
        w2 = jnp.concatenate([wi[:, :HD], wi[:, HD:]], axis=0)
        q2t = q2.T
        w2t = w2.T
        tiles = hi - lo + 1
        chunks = (tiles + 1) // 2

        def body(n):
            st_t = jnp.minimum(lo, nt - 2 * n)
            st = pl.multiple_of(st_t * TILE, TILE)
            W = 2 * TILE
            row = lax.broadcasted_iota(jnp.int32, (TILE, 1), 0)
            row = jnp.concatenate([row, row], axis=0)
            first = lo * TILE - st
            last = jnp.where(img > 0, jnp.full((2 * TILE, 1), (hi + 1) * TILE - 1 - st), r0 - st + row)
            m = None
            for ch in range(n):
                kc = kv[pl.ds(st + ch * W, W), :HD]
                vc = kv[pl.ds(st + ch * W, W), HD:]
                s = lax.dot_general(q2, kc, (((1,), (1,)), ((), ())), preferred_element_type=jnp.float32)
                if ch == 0 or ch == n - 1:
                    col = lax.broadcasted_iota(jnp.int32, (1, W), 1) + ch * W
                    ok = col <= last
                    if ch == 0 or n == 1:
                        ok = ok & (col >= first)
                    s = jnp.where(ok, s, MASKED)
                s_scr[:, ch * W:(ch + 1) * W] = s
                mm = jnp.maximum(s[:, :HD], s[:, HD:])
                m = mm if m is None else jnp.maximum(m, mm)
                dp_scr[:, ch * W:(ch + 1) * W] = lax.dot_general(w2, vc, (((1,), (1,)), ((), ())), preferred_element_type=jnp.float32)
            mr = jnp.max(m, axis=1, keepdims=True) * c2
            l = None
            for ch in range(n):
                p = jnp.exp2(s_scr[:, ch * W:(ch + 1) * W] * c2 - mr)
                s_scr[:, ch * W:(ch + 1) * W] = p
                pd = p * dp_scr[:, ch * W:(ch + 1) * W]
                ll = p[:, :HD] + p[:, HD:]
                rr = pd[:, :HD] + pd[:, HD:]
                l = ll if l is None else l + ll
                r = rr if ch == 0 else r + rr
            inv = 1.0 / jnp.sum(l, axis=1, keepdims=True)
            rd = jnp.sum(r, axis=1, keepdims=True) * inv
            dq = None
            for ch in range(n):
                kc = kv[pl.ds(st + ch * W, W), :HD]
                at = s_scr[:, ch * W:(ch + 1) * W] * inv
                ds = (at * (dp_scr[:, ch * W:(ch + 1) * W] - rd)).astype(jnp.bfloat16)
                at = at.astype(jnp.bfloat16)
                d = jnp.dot(ds, kc, preferred_element_type=jnp.float32)
                dq = d if dq is None else dq + d
                cols = pl.ds(st + ch * W, W)
                acc[:HD, cols] += jnp.dot(q2t, ds, preferred_element_type=jnp.float32)
                acc[HD:, cols] += jnp.dot(w2t, at, preferred_element_type=jnp.float32)
            dq = (dq * inv_root).astype(jnp.bfloat16)
            dq_ref[0, pl.ds(r0, TILE), :HD] = dq[:TILE]
            dq_ref[0, pl.ds(r0, TILE), HD:] = dq[TILE:]

        for n in range(1, nt // 2 + 1):
            @pl.when(chunks == n)
            def _():
                body(n)
        return carry

    lax.fori_loop(0, nt, row_tile, 0)
    kvt_ref[:HD] = (acc[:HD] * inv_root).astype(jnp.bfloat16)
    kvt_ref[HD:] = acc[HD:].astype(jnp.bfloat16)


def attention(queries, out_grad, key_values, ratio, pair, item, image):
    L = queries.shape[1]
    nt = L // TILE
    smem = pl.BlockSpec(memory_space=pltpu.SMEM)
    vmem = pl.BlockSpec(memory_space=pltpu.VMEM)
    return pl.pallas_call(
        attention_kernel,
        out_shape=[jax.ShapeDtypeStruct(queries.shape, jnp.bfloat16),
                   jax.ShapeDtypeStruct((2 * HD, L), jnp.bfloat16)],
        in_specs=[smem] * 4 + [vmem, vmem, pl.BlockSpec(memory_space=pl.ANY)],
        out_specs=[vmem, vmem],
        scratch_shapes=[
            pltpu.VMEM((L, 2 * HD), jnp.bfloat16),
            pltpu.VMEM((2 * TILE, L), jnp.float32),
            pltpu.VMEM((2 * TILE, L), jnp.float32),
            pltpu.VMEM((2 * HD, L), jnp.float32),
            pltpu.SMEM((nt,), jnp.int32),
            pltpu.SMEM((nt,), jnp.int32),
            pltpu.SMEM((2 * ratio.shape[1],), jnp.float32),
            pltpu.SemaphoreType.DMA,
        ],
        compiler_params=pltpu.CompilerParams(vmem_limit_bytes=48 << 20),
        cost_estimate=pl.CostEstimate(flops=10 * 10**9, bytes_accessed=8 << 20, transcendentals=0),
        name="attention",
    )(ratio, pair, item, image, queries, out_grad, key_values)


CHUNKS = 4
MESH = pl.DeviceIdType.MESH


def exchange_kernel(kvt, x_own, x1, x2, x3, x4, x5, x6, x7, out_ref,
                    own, core_in, part, z_in, heads, xs, stage, landed,
                    core_s, core_r, z_s, z_r, right_s, right_r, left_s, left_r,
                    fr_s, fr_r, fl_s, fl_r, xs_s, xs_r, load_sem, x_sem, out_s, out_r):
    dp = lax.axis_index("dp")
    tp = lax.axis_index("tp")
    x = tp // 4
    zl = tp // 2 % 2
    c = tp % 2
    place = tp // 2
    half = 2 * HD // 2
    rows = half // CHUNKS
    length = heads.shape[2]
    cols = xs.shape[3]
    sibling = x * 4 + zl * 2 + (1 - c)
    across = x * 4 + (1 - zl) * 2 + c
    right = lax.rem(x + 1, 4) * 4 + zl * 2 + c
    left = lax.rem(x + 3, 4) * 4 + zl * 2 + c

    load = pltpu.make_async_copy(kvt.at[pl.ds(pl.multiple_of(c * half, half), half)], own, load_sem)
    load.start()
    x_loads = []
    sources = (x_own, x1, x2, x3, x4, x5, x6, x7)
    for i, src in enumerate(sources):
        dx, dz = i // 2, i % 2
        j = lax.rem(x + 4 - dx, 4) * 2 + lax.rem(zl + dz, 2)
        if i == 0:
            src = src.at[:, pl.ds(pl.multiple_of(place * cols, cols), cols)]
        cp = pltpu.make_async_copy(src, xs.at[j, c], x_sem.at[i])
        cp.start()
        x_loads.append(cp)

    barrier = pltpu.get_barrier_semaphore()
    for partner in (sibling, across, right, left):
        pl.semaphore_signal(barrier, 1, device_id=(dp, partner), device_id_type=MESH)

    def dest(k, h, e):
        return place * 2 + e, h * 4 + c * 2 + k // 2

    def greet_dest(i, n):
        u, h, e = i // 8, i // 2 % 4, i % 2
        d, t = dest(u * 2, h, e)
        other = jnp.logical_or(d != dp, t != tp)

        @pl.when(other)
        def _():
            pl.semaphore_signal(barrier, 1, device_id=(d, t), device_id_type=MESH)
        return n + jnp.where(other, 1, 0)

    src_tp = (dp // 4) * 4 + (dp % 4 // 2) * 2 + zl

    def greet_source(i, n):
        other = jnp.logical_or(i != dp, src_tp != tp)

        @pl.when(other)
        def _():
            pl.semaphore_signal(barrier, 1, device_id=(i, src_tp), device_id_type=MESH)
        return n + jnp.where(other, 1, 0)

    n = lax.fori_loop(0, 16, greet_dest, jnp.int32(4))
    n = lax.fori_loop(0, 16, greet_source, n)
    pl.semaphore_wait(barrier, n)

    def remote(src, dst, ss, rs, t):
        return pltpu.make_async_remote_copy(src_ref=src, dst_ref=dst, send_sem=ss, recv_sem=rs,
                                            device_id=(dp, t), device_id_type=MESH)

    def cut(k):
        return pl.ds(k * rows, rows)

    core = []
    for k in range(CHUNKS):
        base = pl.multiple_of((1 - c) * half, half)
        cp = remote(kvt.at[pl.ds(base + k * rows, rows)], core_in.at[cut(k)], core_s.at[k], core_r.at[k], sibling)
        cp.start()
        core.append(cp)
    for cp in x_loads:
        cp.wait()
    x_send = remote(xs.at[:, c], xs.at[:, c], xs_s, xs_r, sibling)
    x_send.start()
    load.wait()

    zc, rc, lc, frc, flc = [], [], [], [], []

    def reduce_core(k):
        core[k].wait_recv()
        part[cut(k)] = (own[cut(k)].astype(jnp.float32) + core_in[cut(k)].astype(jnp.float32)).astype(jnp.bfloat16)
        cp = remote(part.at[cut(k)], z_in.at[cut(k)], z_s.at[k], z_r.at[k], across)
        cp.start()
        zc.append(cp)

    def reduce_z(k):
        zc[k].wait_recv()
        heads[x, cut(k)] = (part[cut(k)].astype(jnp.float32) + z_in[cut(k)].astype(jnp.float32)).astype(jnp.bfloat16)
        here = heads.at[x, cut(k)]
        for lst, ss, rs, t in ((rc, right_s, right_r, right), (lc, left_s, left_r, left)):
            cp = remote(here, here, ss.at[k], rs.at[k], t)
            cp.start()
            lst.append(cp)

    def forward(k):
        rc[k].wait_recv()
        a = heads.at[lax.rem(x + 3, 4), cut(k), pl.ds(0, length // 2)]
        cp = remote(a, a, fr_s.at[k], fr_r.at[k], right)
        cp.start()
        frc.append(cp)
        lc[k].wait_recv()
        b = heads.at[lax.rem(x + 1, 4), cut(k), pl.ds(length // 2, length // 2)]
        cp = remote(b, b, fl_s.at[k], fl_r.at[k], left)
        cp.start()
        flc.append(cp)

    def out_copy(k, i, d, t):
        h, e = i // 2, i % 2
        return pltpu.make_async_remote_copy(
            src_ref=stage.at[k, h, e], dst_ref=landed.at[dp, k % 2], send_sem=out_s.at[k * 8 + i],
            recv_sem=out_r.at[dp, k % 2], device_id=(d, t), device_id_type=MESH)

    def multiply(k):
        frc[k].wait_recv()
        flc[k].wait_recv()
        if k == 0:
            x_send.wait_recv()
        lhs = heads[:, k * rows:(k + 1) * rows, :].reshape(4 * rows, length)
        res = jnp.dot(lhs, xs[...].reshape(length, cols), preferred_element_type=jnp.float32)
        res = res.astype(jnp.bfloat16).reshape(4, rows, cols)
        for e in range(2):
            stage[k, :, e] = res[:, :, e * (cols // 2):(e + 1) * (cols // 2)]

        def send(i, carry):
            d, t = dest(k, i // 2, i % 2)
            other = jnp.logical_or(d != dp, t != tp)

            @pl.when(other)
            def _():
                out_copy(k, i, d, t).start()

            @pl.when(jnp.logical_not(other))
            def _():
                pltpu.make_async_copy(stage.at[k, i // 2, i % 2], landed.at[dp, k % 2], out_r.at[dp, k % 2]).start()
            return carry
        lax.fori_loop(0, 8, send, 0)

    for step in range(CHUNKS + 3):
        if step < CHUNKS:
            reduce_core(step)
        if 0 <= step - 1 < CHUNKS:
            reduce_z(step - 1)
        if 0 <= step - 2 < CHUNKS:
            forward(step - 2)
        if 0 <= step - 3 < CHUNKS:
            multiply(step - 3)

    def collect(i, total):
        new = []
        for p in range(2):
            pltpu.make_async_copy(landed.at[i, p], landed.at[i, p], out_r.at[i, p]).wait()
            new.append(total[p] + landed[i, p].astype(jnp.float32))
        return tuple(new)

    zero = jnp.zeros((rows, cols // 2), jnp.float32)
    top, bottom = lax.fori_loop(0, 16, collect, (zero, zero))
    out_ref[:rows] = top
    out_ref[rows:] = bottom

    for group in (core, zc, rc, lc, frc, flc, [x_send]):
        for cp in group:
            cp.wait_send()

    def drain(j, carry):
        k, i = j // 8, j % 8
        d, t = dest(k, i // 2, i % 2)

        @pl.when(jnp.logical_or(d != dp, t != tp))
        def _():
            out_copy(k, i, d, t).wait_send()
        return carry
    lax.fori_loop(0, 8 * CHUNKS, drain, 0)


def exchange(kvt, x_own, others):
    length = kvt.shape[1]
    cols = others[0].shape[1]
    half = HD
    rows = half // CHUNKS
    sem = pltpu.SemaphoreType.DMA
    bf = jnp.bfloat16
    return pl.pallas_call(
        exchange_kernel,
        out_shape=jax.ShapeDtypeStruct((2 * rows, cols // 2), jnp.float32),
        in_specs=[pl.BlockSpec(memory_space=pl.ANY)] * 9,
        out_specs=pl.BlockSpec(memory_space=pltpu.VMEM),
        scratch_shapes=[
            pltpu.VMEM((half, length), bf), pltpu.VMEM((half, length), bf),
            pltpu.VMEM((half, length), bf), pltpu.VMEM((half, length), bf),
            pltpu.VMEM((4, half, length), bf), pltpu.VMEM((8, 2, TILE, cols), bf),
            pltpu.VMEM((CHUNKS, 4, 2, rows, cols // 2), bf), pltpu.VMEM((16, 2, rows, cols // 2), bf),
        ] + [sem((CHUNKS,))] * 12 + [sem, sem, sem, sem((8,)), sem((8 * CHUNKS,)), sem((16, 2))],
        compiler_params=pltpu.CompilerParams(collective_id=0, has_side_effects=True, vmem_limit_bytes=48 << 20),
        cost_estimate=pl.CostEstimate(flops=10**9, bytes_accessed=8 << 20, transcendentals=0),
        name="exchange",
    )(kvt, x_own, *others)


def local(input_rows, queries, key_values, out_grad, item_logratio, pair_ids, tile_item, tile_image):
    t = lax.axis_index("tp")
    rows = input_rows[0]
    cols = rows.shape[1] // 8
    others = []
    for i in range(1, 8):
        dx, dz = i // 2, i % 2
        to = (t // 4 + dx) % 4 * 2 + (t // 2 + dz) % 2
        pairs = [(a, (a // 4 + dx) % 4 * 4 + (a // 2 + dz) % 2 * 2 + a % 2) for a in range(16)]
        others.append(lax.ppermute(lax.dynamic_slice_in_dim(rows, to * cols, cols, 1), "tp", pairs))
    dq, kvt = attention(queries, out_grad, key_values, item_logratio, pair_ids, tile_item, tile_image)
    return dq, exchange(kvt, rows, others).T


def solution(mesh):
    in_specs = (P("dp", "tp", None), P("dp", None, "tp"), P("dp", None, None), P("dp", None, "tp"),
                P("dp", None), P("dp", None), P("dp", None), P("dp", None))
    out_specs = (P("dp", None, "tp"), P("dp", "tp"))
    return jax.shard_map(local, mesh=mesh, in_specs=in_specs, out_specs=out_specs, check_vma=False)
```

```python
import functools, math
import jax, jax.numpy as jnp
from jax import lax
from jax.experimental import pallas as pl
from jax.experimental.pallas import tpu as pltpu

from jax.sharding import PartitionSpec as P

KVH = 4; HD = 128; TILE = 128; BETA = 0.1
MASKED = -1e30
LOG2E = 1.4426950408889634

def attention_kernel(ratio_h, pair_h, item_h, image_h, q_hbm, og_hbm, kv_hbm, dq_hbm, kvt_ref,
                     kv, q_ref, og_ref, dq_ref, s0, s1, dp0, dp1, acc, ratio, pair, item, image,
                     lo_s, hi_s, z_s, small_sem, big_sem, dq_sem):
    group = lax.axis_size("tp") // KVH
    g = lax.axis_index("tp") // group
    nt = item.shape[1]
    items = ratio.shape[1]
    small = [pltpu.make_async_copy(a, b, small_sem.at[i])
             for i, (a, b) in enumerate(((ratio_h, ratio), (pair_h, pair), (item_h, item), (image_h, image)))]
    for cp in small:
        cp.start()
    big = [pltpu.make_async_copy(kv_hbm.at[0, :, pl.ds(pl.multiple_of(g * 2 * HD, 2 * HD), 2 * HD)], kv, big_sem.at[0]),
           pltpu.make_async_copy(q_hbm.at[0], q_ref, big_sem.at[1]),
           pltpu.make_async_copy(og_hbm.at[0], og_ref, big_sem.at[2])]
    for cp in big:
        cp.start()
    inv_root = 1.0 / math.sqrt(HD)
    c2 = inv_root * LOG2E
    W = 2 * TILE
    acc[...] = jnp.zeros_like(acc)
    for cp in small:
        cp.wait()
    lo_s[0] = 0
    for i in range(1, nt):
        lo_s[i] = jnp.where(item[0, i] == item[0, i - 1], lo_s[i - 1], i)
    hi_s[nt - 1] = nt - 1
    for i in reversed(range(nt - 1)):
        same = (image[0, i] > 0) & (image[0, i] == image[0, i + 1]) & (item[0, i] == item[0, i + 1])
        hi_s[i] = jnp.where(same, hi_s[i + 1], i)
    for a in range(items):
        other = jnp.float32(0.0)
        p = jnp.float32(1.0)
        for b in range(items):
            if b != a:
                same = pair[0, a] == pair[0, b]
                other = other + jnp.where(same, ratio[0, b], 0.0)
                if a < b:
                    p = jnp.where(same, -1.0, p)
        z_s[a] = BETA * p * (other - ratio[0, a])
        z_s[items + a] = p
    for cp in big:
        cp.wait()

    def block(I, n, spare, s_scr, dp_scr):
        lo = lo_s[I]
        hi = hi_s[I]
        img = image[0, I]
        it = item[0, I]
        r0 = pl.multiple_of(I * TILE, TILE)
        st = pl.multiple_of(jnp.clip(hi + 1 - 2 * n, 0, nt - 2 * n) * TILE, TILE)
        first = lo * TILE - st
        v = {}

        def stage1():
            qi = q_ref[pl.ds(r0, TILE), :]
            q2 = jnp.concatenate([qi[:, :HD], qi[:, HD:]], axis=0)
            coef = z_s[items + it] / (1.0 + jnp.exp(jnp.full((8, HD), z_s[it], jnp.float32)))
            coef = jnp.concatenate([coef[:1], coef[:1]], axis=1)
            wi = (og_ref[pl.ds(r0, TILE), :].astype(jnp.float32) * coef).astype(jnp.bfloat16)
            w2 = jnp.concatenate([wi[:, :HD], wi[:, HD:]], axis=0)
            v["q2t"] = q2.T
            v["w2t"] = w2.T
            row = lax.broadcasted_iota(jnp.int32, (TILE, 1), 0)
            row = jnp.concatenate([row, row], axis=0)
            last = jnp.where(img > 0, jnp.full((2 * TILE, 1), (hi + 1) * TILE - 1 - st), r0 - st + row)
            m = None
            for ch in range(n):
                rows = pl.ds(st + ch * W, W)
                s = lax.dot_general(q2, kv[rows, :HD], (((1,), (1,)), ((), ())), preferred_element_type=jnp.float32)
                if ch <= spare or ch == n - 1:
                    col = lax.broadcasted_iota(jnp.int32, (1, W), 1) + ch * W
                    ok = (col <= last) & (col >= first)
                    s = jnp.where(ok, s, MASKED)
                s_scr[:, ch * W:(ch + 1) * W] = s
                mm = jnp.maximum(s[:, :HD], s[:, HD:])
                m = mm if m is None else jnp.maximum(m, mm)
                dp_scr[:, ch * W:(ch + 1) * W] = lax.dot_general(
                    w2, kv[rows, HD:], (((1,), (1,)), ((), ())), preferred_element_type=jnp.float32)
            v["m"] = jnp.max(m, axis=1, keepdims=True) * c2

        def stage2():
            mr = v["m"]
            l = r = None
            for ch in range(n):
                cols = slice(ch * W, (ch + 1) * W)
                p = jnp.exp2(s_scr[:, cols] * c2 - mr)
                s_scr[:, cols] = p
                pd = p * dp_scr[:, cols]
                ll = p[:, :HD] + p[:, HD:]
                rr = pd[:, :HD] + pd[:, HD:]
                l = ll if l is None else l + ll
                r = rr if r is None else r + rr
            v["inv"] = 1.0 / jnp.sum(l, axis=1, keepdims=True)
            v["rd"] = jnp.sum(r, axis=1, keepdims=True) * v["inv"]

        def stage3():
            inv, rd = v["inv"], v["rd"]
            dq = None
            for ch in range(n):
                rows = pl.ds(st + ch * W, W)
                cols = slice(ch * W, (ch + 1) * W)
                at = s_scr[:, cols] * inv
                ds = (at * (dp_scr[:, cols] - rd)).astype(jnp.bfloat16)
                at = at.astype(jnp.bfloat16)
                d = jnp.dot(ds, kv[rows, :HD], preferred_element_type=jnp.float32)
                dq = d if dq is None else dq + d
                acc[:HD, rows] += jnp.dot(v["q2t"], ds, preferred_element_type=jnp.float32)
                acc[HD:, rows] += jnp.dot(v["w2t"], at, preferred_element_type=jnp.float32)
            dq = (dq * inv_root).astype(jnp.bfloat16)
            dq_ref[pl.ds(r0, TILE), :HD] = dq[:TILE]
            dq_ref[pl.ds(r0, TILE), HD:] = dq[TILE:]

        return stage1, stage2, stage3

    def chunks(I):
        return (hi_s[I] - lo_s[I] + 2) // 2

    def single(I):
        n_here = chunks(I)
        for n in range(1, nt // 2 + 1):
            @pl.when(n_here == n)
            def _():
                for stage in block(I, n, 0, s0, dp0):
                    stage()

    def row_pair(j, carry):
        a = 2 * j
        na, nb = chunks(a), chunks(a + 1)
        most = jnp.maximum(na, nb)
        near = most - jnp.minimum(na, nb) <= 1
        for n in range(1, nt // 2 + 1):
            @pl.when(near & (most == n))
            def _():
                one = block(a, n, 1, s0, dp0)
                two = block(a + 1, n, 1, s1, dp1)
                for f, g2 in zip(one, two):
                    f()
                    g2()

        @pl.when(jnp.logical_not(near))
        def _():
            def each(i, c):
                single(a + i)
                return c
            lax.fori_loop(0, 2, each, 0)
        here = pl.ds(pl.multiple_of(j * 2 * TILE, 2 * TILE), 2 * TILE)
        pltpu.make_async_copy(dq_ref.at[here], dq_hbm.at[0, here], dq_sem.at[j]).start()
        return carry

    lax.fori_loop(0, nt // 2, row_pair, 0)
    for i in range(nt // 4):
        for z in range(2):
            frm = slice((2 * i + z) * W, (2 * i + z + 1) * W)
            to = slice(i * W, (i + 1) * W)
            kvt_ref[0, z, :, to] = (acc[:HD, frm] * inv_root).astype(jnp.bfloat16)
            kvt_ref[1, z, :, to] = acc[HD:, frm].astype(jnp.bfloat16)

    def finish(j, carry):
        here = pl.ds(pl.multiple_of(j * 2 * TILE, 2 * TILE), 2 * TILE)
        pltpu.make_async_copy(dq_ref.at[here], dq_hbm.at[0, here], dq_sem.at[j]).wait()
        return carry
    lax.fori_loop(0, nt // 2, finish, 0)


def attention(queries, out_grad, key_values, ratio, pair, item, image):
    L = queries.shape[1]
    nt = L // TILE
    hbm = pl.BlockSpec(memory_space=pl.ANY)
    wide = pltpu.VMEM((2 * TILE, L), jnp.float32)
    low = pltpu.VMEM((L, 2 * HD), jnp.bfloat16)
    return pl.pallas_call(
        attention_kernel,
        out_shape=[jax.ShapeDtypeStruct(queries.shape, jnp.bfloat16),
                   jax.ShapeDtypeStruct((2, 2, HD, L // 2), jnp.bfloat16)],
        in_specs=[hbm] * 7,
        out_specs=[hbm, pl.BlockSpec(memory_space=pltpu.VMEM)],
        scratch_shapes=[low, low, low, low, wide, wide, wide, wide,
            pltpu.VMEM((2 * HD, L), jnp.float32),
            pltpu.SMEM(ratio.shape, jnp.float32),
            pltpu.SMEM(pair.shape, jnp.int32),
            pltpu.SMEM(item.shape, jnp.int32),
            pltpu.SMEM(image.shape, jnp.int32),
            pltpu.SMEM((nt,), jnp.int32),
            pltpu.SMEM((nt,), jnp.int32),
            pltpu.SMEM((2 * ratio.shape[1],), jnp.float32),
            pltpu.SemaphoreType.DMA((4,)), pltpu.SemaphoreType.DMA((3,)), pltpu.SemaphoreType.DMA((nt // 2,)),
        ],
        compiler_params=pltpu.CompilerParams(vmem_limit_bytes=56 << 20),
        cost_estimate=pl.CostEstimate(flops=10 * 10**9, bytes_accessed=8 << 20, transcendentals=0),
        name="attention",
    )(ratio, pair, item, image, queries, out_grad, key_values)


CHUNKS = 4
PARTS = CHUNKS // 2
MESH = pl.DeviceIdType.MESH
F32 = jnp.float32
BF16 = jnp.bfloat16


def exchange_kernel(kvt, x_own, x1, x2, x3, out_ref,
                    own, core_in, part, z_in, heads, xs, prod, y1_out, y1_in, y2_out, y2_in, final, landed,
                    core_s, core_r, z_s, z_r, right_s, right_r, left_s, left_r,
                    fr_s, fr_r, fl_s, fl_r, y1r_s, y1r_r, y1l_s, y1l_r, y2r_s, y2r_r, y2l_s, y2l_r,
                    xs_s, xs_r, load_sem, x_sem, out_s, out_r):
    dp = lax.axis_index("dp")
    tp = lax.axis_index("tp")
    y = dp // 4
    zh = dp % 4
    x = tp // 4
    zl = tp // 2 % 2
    c = tp % 2
    rows, length = z_in.shape[1:]
    cols = xs.shape[3]
    half = length // 2
    mid = cols // 2
    sibling = (dp, x * 4 + zl * 2 + (1 - c))
    across = (dp, x * 4 + (1 - zl) * 2 + c)
    right = (dp, lax.rem(x + 1, 4) * 4 + zl * 2 + c)
    left = (dp, lax.rem(x + 3, 4) * 4 + zl * 2 + c)
    above = (lax.rem(y + 1, 4) * 4 + zh, tp)
    below = (lax.rem(y + 3, 4) * 4 + zh, tp)

    load = pltpu.make_async_copy(kvt.at[c], own, load_sem)
    load.start()
    x_loads = []
    for i, src in enumerate((x_own, x1, x2, x3)):
        if i == 0:
            src = src.at[:, pl.ds(pl.multiple_of(x * cols, cols), cols)]
        cp = pltpu.make_async_copy(src, xs.at[lax.rem(x + 4 - i, 4), c], x_sem.at[i])
        cp.start()
        x_loads.append(cp)

    barrier = pltpu.get_barrier_semaphore()
    for partner in (sibling, across, right, left, above, below):
        pl.semaphore_signal(barrier, 1, device_id=partner, device_id_type=MESH)

    def dest(u, q):
        return x * 4 + q, y * 4 + c * 2 + u

    def is_other(d, t):
        return jnp.logical_or(d != dp, t != tp)

    def greet(d, t, n):
        other = is_other(d, t)

        @pl.when(other)
        def _():
            pl.semaphore_signal(barrier, 1, device_id=(d, t), device_id_type=MESH)
        return n + jnp.where(other, 1, 0)

    n = lax.fori_loop(0, 8, lambda i, n: greet(*dest(i // 4, i % 4), n), jnp.int32(6))
    n = lax.fori_loop(0, 8, lambda i, n: greet(x * 4 + i // 2, y * 4 + i % 2 * 2 + zl, n), n)
    pl.semaphore_wait(barrier, n)

    started = []

    def send(src, dst, ss, rs, to):
        cp = pltpu.make_async_remote_copy(src_ref=src, dst_ref=dst, send_sem=ss, recv_sem=rs,
                                          device_id=to, device_id_type=MESH)
        cp.start()
        started.append(cp)
        return cp

    def cut(k):
        return pl.ds(k * rows, rows)

    core = [send(kvt.at[1 - c, :, cut(k)], core_in.at[k], core_s.at[k], core_r.at[k], sibling)
            for k in range(CHUNKS)]
    for cp in x_loads:
        cp.wait()
    x_send = send(xs.at[:, c], xs.at[:, c], xs_s, xs_r, sibling)
    load.wait()

    zc, rc, lc, frc, flc, y1r, y1l, y2r, y2l = ([] for _ in range(9))

    def reduce_core(k):
        core[k].wait_recv()
        part[k] = (own[1 - zl, cut(k)].astype(F32) + core_in[k, 1 - zl].astype(F32)).astype(BF16)
        zc.append(send(part.at[k], z_in.at[k], z_s.at[k], z_r.at[k], across))

    def reduce_z(k):
        zc[k].wait_recv()
        heads[k, x] = (own[zl, cut(k)].astype(F32) + core_in[k, zl].astype(F32) + z_in[k].astype(F32)).astype(BF16)
        here = heads.at[k, x]
        rc.append(send(here, here, right_s.at[k], right_r.at[k], right))
        lc.append(send(here, here, left_s.at[k], left_r.at[k], left))

    def forward(k):
        rc[k].wait_recv()
        a = heads.at[k, lax.rem(x + 3, 4), :, pl.ds(0, half)]
        frc.append(send(a, a, fr_s.at[k], fr_r.at[k], right))
        lc[k].wait_recv()
        b = heads.at[k, lax.rem(x + 1, 4), :, pl.ds(half, half)]
        flc.append(send(b, b, fl_s.at[k], fl_r.at[k], left))

    def multiply(k):
        frc[k].wait_recv()
        flc[k].wait_recv()
        if k == 0:
            x_send.wait_recv()
        lhs = heads[k].reshape(4 * rows, length)
        prod[k] = jnp.dot(lhs, xs[...].reshape(length, cols), preferred_element_type=F32).reshape(4, rows, cols)
        far = prod[k, lax.rem(y + 2, 4)].astype(BF16)
        y1_out[k, 0] = far[:, :mid]
        y1_out[k, 1] = far[:, mid:]
        y1r.append(send(y1_out.at[k, 0], y1_in.at[k, 0], y1r_s.at[k], y1r_r.at[k], above))
        y1l.append(send(y1_out.at[k, 1], y1_in.at[k, 1], y1l_s.at[k], y1l_r.at[k], below))

    def pass_on(k):
        y1r[k].wait_recv()
        mine = prod[k, lax.rem(y + 1, 4)]
        y2_out[k, 0, :, :mid] = (mine[:, :mid] + y1_in[k, 0].astype(F32)).astype(BF16)
        y2_out[k, 0, :, mid:] = mine[:, mid:].astype(BF16)
        y2r.append(send(y2_out.at[k, 0], y2_in.at[k, 0], y2r_s.at[k], y2r_r.at[k], above))
        y1l[k].wait_recv()
        mine = prod[k, lax.rem(y + 3, 4)]
        y2_out[k, 1, :, :mid] = mine[:, :mid].astype(BF16)
        y2_out[k, 1, :, mid:] = (mine[:, mid:] + y1_in[k, 1].astype(F32)).astype(BF16)
        y2l.append(send(y2_out.at[k, 1], y2_in.at[k, 1], y2l_s.at[k], y2l_r.at[k], below))

    spot = zh * 2 + zl

    def out_copy(k, q):
        d, t = dest(k // PARTS, q)
        return d, t, pltpu.make_async_remote_copy(
            src_ref=final.at[k, q], dst_ref=landed.at[spot, k % PARTS], send_sem=out_s.at[k * 4 + q],
            recv_sem=out_r.at[spot, k % PARTS], device_id=(d, t), device_id_type=MESH)

    def deliver(k):
        y2r[k].wait_recv()
        y2l[k].wait_recv()
        total = (prod[k, y] + y2_in[k, 0].astype(F32) + y2_in[k, 1].astype(F32)).astype(BF16)
        for q in range(4):
            final[k, q] = total[:, q * (cols // 4):(q + 1) * (cols // 4)]

        def one(q, carry):
            d, t, cp = out_copy(k, q)
            other = is_other(d, t)

            @pl.when(other)
            def _():
                cp.start()

            @pl.when(jnp.logical_not(other))
            def _():
                pltpu.make_async_copy(final.at[k, q], landed.at[spot, k % PARTS], out_r.at[spot, k % PARTS]).start()
            return carry
        lax.fori_loop(0, 4, one, 0)

    stages = (reduce_core, reduce_z, forward, multiply, pass_on, deliver)
    for step in range(CHUNKS + len(stages) - 1):
        for i, stage in enumerate(stages):
            if 0 <= step - i < CHUNKS:
                stage(step - i)

    def collect(i, total):
        new = []
        for p in range(PARTS):
            pltpu.make_async_copy(landed.at[i, p], landed.at[i, p], out_r.at[i, p]).wait()
            new.append(total[p] + landed[i, p].astype(F32))
        return tuple(new)

    zero = jnp.zeros((rows, cols // 4), F32)
    sums = lax.fori_loop(0, 8, collect, (zero,) * PARTS)
    for p in range(PARTS):
        out_ref[p * rows:(p + 1) * rows] = sums[p]

    for cp in started:
        cp.wait_send()

    def drain(j, carry):
        d, t, cp = out_copy(j // 4, j % 4)

        @pl.when(is_other(d, t))
        def _():
            cp.wait_send()
        return carry
    lax.fori_loop(0, 4 * CHUNKS, drain, 0)


def exchange(kvt, x_own, others):
    length = kvt.shape[3]
    cols = others[0].shape[1]
    rows = HD // CHUNKS
    sem = pltpu.SemaphoreType.DMA
    n = CHUNKS
    return pl.pallas_call(
        exchange_kernel,
        out_shape=jax.ShapeDtypeStruct((PARTS * rows, cols // 4), F32),
        in_specs=[pl.BlockSpec(memory_space=pl.ANY)] * 5,
        out_specs=pl.BlockSpec(memory_space=pltpu.VMEM),
        scratch_shapes=[
            pltpu.VMEM((2, HD, length), BF16), pltpu.VMEM((n, 2, rows, length), BF16),
            pltpu.VMEM((n, rows, length), BF16), pltpu.VMEM((n, rows, length), BF16),
            pltpu.VMEM((n, 4, rows, length), BF16), pltpu.VMEM((4, 2, TILE, cols), BF16),
            pltpu.VMEM((n, 4, rows, cols), F32),
            pltpu.VMEM((n, 2, rows, cols // 2), BF16), pltpu.VMEM((n, 2, rows, cols // 2), BF16),
            pltpu.VMEM((n, 2, rows, cols), BF16), pltpu.VMEM((n, 2, rows, cols), BF16),
            pltpu.VMEM((n, 4, rows, cols // 4), BF16), pltpu.VMEM((8, PARTS, rows, cols // 4), BF16),
        ] + [sem((n,))] * 20 + [sem, sem, sem, sem((4,)), sem((4 * n,)), sem((8, PARTS))],
        compiler_params=pltpu.CompilerParams(collective_id=0, has_side_effects=True, vmem_limit_bytes=56 << 20),
        cost_estimate=pl.CostEstimate(flops=10**9, bytes_accessed=8 << 20, transcendentals=0),
        name="exchange",
    )(kvt, x_own, *others)


def local(input_rows, queries, key_values, out_grad, item_logratio, pair_ids, tile_item, tile_image):
    t = lax.axis_index("tp")
    rows = input_rows[0]
    cols = rows.shape[1] // 4
    others = []
    for dx in range(1, 4):
        to = (t // 4 + dx) % 4
        pairs = [(a, (a + 4 * dx) % 16) for a in range(16)]
        others.append(lax.ppermute(lax.dynamic_slice_in_dim(rows, to * cols, cols, 1), "tp", pairs))
    dq, kvt = attention(queries, out_grad, key_values, item_logratio, pair_ids, tile_item, tile_image)
    return dq, exchange(kvt, rows, others).T


def solution(mesh):
    in_specs = (P("dp", "tp", None), P("dp", None, "tp"), P("dp", None, None), P("dp", None, "tp"),
                P("dp", None), P("dp", None), P("dp", None), P("dp", None))
    out_specs = (P("dp", None, "tp"), P("dp", "tp"))
    return jax.shard_map(local, mesh=mesh, in_specs=in_specs, out_specs=out_specs, check_vma=False)
```

```python
import functools, math
import jax, jax.numpy as jnp
from jax import lax
from jax.experimental import pallas as pl
from jax.experimental.pallas import tpu as pltpu

from jax.sharding import PartitionSpec as P

KVH = 4; HD = 128; TILE = 128; BETA = 0.1
MASKED = -1e30
LOG2E = 1.4426950408889634

def attention_kernel(ratio_h, pair_h, item_h, image_h, q_hbm, og_hbm, kv_hbm, dq_hbm, kvt_ref,
                     kv, q_ref, og_ref, dq_ref, s0, s1, dp0, dp1, acc, ratio, pair, item, image,
                     lo_s, hi_s, z_s, small_sem, big_sem, dq_sem):
    group = lax.axis_size("tp") // KVH
    g = lax.axis_index("tp") // group
    nt = item.shape[1]
    items = ratio.shape[1]
    small = [pltpu.make_async_copy(a, b, small_sem.at[i])
             for i, (a, b) in enumerate(((ratio_h, ratio), (pair_h, pair), (item_h, item), (image_h, image)))]
    for cp in small:
        cp.start()
    big = [pltpu.make_async_copy(kv_hbm.at[0, :, pl.ds(pl.multiple_of(g * 2 * HD, 2 * HD), 2 * HD)], kv, big_sem.at[0]),
           pltpu.make_async_copy(q_hbm.at[0], q_ref, big_sem.at[1]),
           pltpu.make_async_copy(og_hbm.at[0], og_ref, big_sem.at[2])]
    for cp in big:
        cp.start()
    inv_root = 1.0 / math.sqrt(HD)
    c2 = inv_root * LOG2E
    W = 2 * TILE
    acc[...] = jnp.zeros_like(acc)
    for cp in small:
        cp.wait()
    lo_s[0] = 0
    for i in range(1, nt):
        lo_s[i] = jnp.where(item[0, i] == item[0, i - 1], lo_s[i - 1], i)
    hi_s[nt - 1] = nt - 1
    for i in reversed(range(nt - 1)):
        same = (image[0, i] > 0) & (image[0, i] == image[0, i + 1]) & (item[0, i] == item[0, i + 1])
        hi_s[i] = jnp.where(same, hi_s[i + 1], i)
    for a in range(items):
        other = jnp.float32(0.0)
        p = jnp.float32(1.0)
        for b in range(items):
            if b != a:
                same = pair[0, a] == pair[0, b]
                other = other + jnp.where(same, ratio[0, b], 0.0)
                if a < b:
                    p = jnp.where(same, -1.0, p)
        z_s[a] = BETA * p * (other - ratio[0, a])
        z_s[items + a] = p
    for cp in big:
        cp.wait()

    def block(I, n, spare, s_scr, dp_scr):
        lo = lo_s[I]
        hi = hi_s[I]
        img = image[0, I]
        it = item[0, I]
        r0 = pl.multiple_of(I * TILE, TILE)
        st = pl.multiple_of(jnp.clip(hi + 1 - 2 * n, 0, nt - 2 * n) * TILE, TILE)
        first = lo * TILE - st
        v = {}

        def stage1():
            qi = q_ref[pl.ds(r0, TILE), :]
            q2 = jnp.concatenate([qi[:, :HD], qi[:, HD:]], axis=0)
            coef = z_s[items + it] / (1.0 + jnp.exp(jnp.full((8, HD), z_s[it], jnp.float32)))
            coef = jnp.concatenate([coef[:1], coef[:1]], axis=1)
            wi = (og_ref[pl.ds(r0, TILE), :].astype(jnp.float32) * coef).astype(jnp.bfloat16)
            w2 = jnp.concatenate([wi[:, :HD], wi[:, HD:]], axis=0)
            v["q2t"] = q2.T
            v["w2t"] = w2.T
            row = lax.broadcasted_iota(jnp.int32, (TILE, 1), 0)
            row = jnp.concatenate([row, row], axis=0)
            last = jnp.where(img > 0, jnp.full((2 * TILE, 1), (hi + 1) * TILE - 1 - st), r0 - st + row)
            m = None
            for ch in range(n):
                rows = pl.ds(st + ch * W, W)
                s = lax.dot_general(q2, kv[rows, :HD], (((1,), (1,)), ((), ())), preferred_element_type=jnp.float32)
                if ch <= spare or ch == n - 1:
                    col = lax.broadcasted_iota(jnp.int32, (1, W), 1) + ch * W
                    ok = (col <= last) & (col >= first)
                    s = jnp.where(ok, s, MASKED)
                s_scr[:, ch * W:(ch + 1) * W] = s
                mm = jnp.maximum(s[:, :HD], s[:, HD:])
                m = mm if m is None else jnp.maximum(m, mm)
                dp_scr[:, ch * W:(ch + 1) * W] = lax.dot_general(
                    w2, kv[rows, HD:], (((1,), (1,)), ((), ())), preferred_element_type=jnp.float32)
            v["m"] = jnp.max(m, axis=1, keepdims=True) * c2

        def stage2():
            mr = v["m"]
            l = r = None
            for ch in range(n):
                cols = slice(ch * W, (ch + 1) * W)
                p = jnp.exp2(s_scr[:, cols] * c2 - mr)
                s_scr[:, cols] = p
                pd = p * dp_scr[:, cols]
                ll = p[:, :HD] + p[:, HD:]
                rr = pd[:, :HD] + pd[:, HD:]
                l = ll if l is None else l + ll
                r = rr if r is None else r + rr
            v["inv"] = 1.0 / jnp.sum(l, axis=1, keepdims=True)
            v["rd"] = jnp.sum(r, axis=1, keepdims=True) * v["inv"]

        def stage3():
            inv, rd = v["inv"], v["rd"]
            dq = None
            for ch in range(n):
                rows = pl.ds(st + ch * W, W)
                cols = slice(ch * W, (ch + 1) * W)
                at = s_scr[:, cols] * inv
                ds = (at * (dp_scr[:, cols] - rd)).astype(jnp.bfloat16)
                at = at.astype(jnp.bfloat16)
                d = jnp.dot(ds, kv[rows, :HD], preferred_element_type=jnp.float32)
                dq = d if dq is None else dq + d
                acc[:HD, rows] += jnp.dot(v["q2t"], ds, preferred_element_type=jnp.float32)
                acc[HD:, rows] += jnp.dot(v["w2t"], at, preferred_element_type=jnp.float32)
            dq = (dq * inv_root).astype(jnp.bfloat16)
            dq_ref[pl.ds(r0, TILE), :HD] = dq[:TILE]
            dq_ref[pl.ds(r0, TILE), HD:] = dq[TILE:]

        return stage1, stage2, stage3

    def chunks(I):
        return (hi_s[I] - lo_s[I] + 2) // 2

    def single(I):
        n_here = chunks(I)
        for n in range(1, nt // 2 + 1):
            @pl.when(n_here == n)
            def _():
                for stage in block(I, n, 0, s0, dp0):
                    stage()

    def row_pair(j, carry):
        a = 2 * j
        na, nb = chunks(a), chunks(a + 1)
        most = jnp.maximum(na, nb)
        near = most - jnp.minimum(na, nb) <= 1
        for n in range(1, nt // 2 + 1):
            @pl.when(near & (most == n))
            def _():
                one = block(a, n, 1, s0, dp0)
                two = block(a + 1, n, 1, s1, dp1)
                for f, g2 in zip(one, two):
                    f()
                    g2()

        @pl.when(jnp.logical_not(near))
        def _():
            def each(i, c):
                single(a + i)
                return c
            lax.fori_loop(0, 2, each, 0)
        here = pl.ds(pl.multiple_of(j * 2 * TILE, 2 * TILE), 2 * TILE)
        pltpu.make_async_copy(dq_ref.at[here], dq_hbm.at[0, here], dq_sem.at[j]).start()
        return carry

    lax.fori_loop(0, nt // 2, row_pair, 0)
    for i in range(nt // 4):
        for z in range(2):
            frm = slice((2 * i + z) * W, (2 * i + z + 1) * W)
            to = slice(i * W, (i + 1) * W)
            kvt_ref[0, z, :, to] = (acc[:HD, frm] * inv_root).astype(jnp.bfloat16)
            kvt_ref[1, z, :, to] = acc[HD:, frm].astype(jnp.bfloat16)

    def finish(j, carry):
        here = pl.ds(pl.multiple_of(j * 2 * TILE, 2 * TILE), 2 * TILE)
        pltpu.make_async_copy(dq_ref.at[here], dq_hbm.at[0, here], dq_sem.at[j]).wait()
        return carry
    lax.fori_loop(0, nt // 2, finish, 0)


def attention(queries, out_grad, key_values, ratio, pair, item, image):
    L = queries.shape[1]
    nt = L // TILE
    hbm = pl.BlockSpec(memory_space=pl.ANY)
    wide = pltpu.VMEM((2 * TILE, L), jnp.float32)
    low = pltpu.VMEM((L, 2 * HD), jnp.bfloat16)
    return pl.pallas_call(
        attention_kernel,
        out_shape=[jax.ShapeDtypeStruct(queries.shape, jnp.bfloat16),
                   jax.ShapeDtypeStruct((2, 2, HD, L // 2), jnp.bfloat16)],
        in_specs=[hbm] * 7,
        out_specs=[hbm, pl.BlockSpec(memory_space=pltpu.VMEM)],
        scratch_shapes=[low, low, low, low, wide, wide, wide, wide,
            pltpu.VMEM((2 * HD, L), jnp.float32),
            pltpu.SMEM(ratio.shape, jnp.float32),
            pltpu.SMEM(pair.shape, jnp.int32),
            pltpu.SMEM(item.shape, jnp.int32),
            pltpu.SMEM(image.shape, jnp.int32),
            pltpu.SMEM((nt,), jnp.int32),
            pltpu.SMEM((nt,), jnp.int32),
            pltpu.SMEM((2 * ratio.shape[1],), jnp.float32),
            pltpu.SemaphoreType.DMA((4,)), pltpu.SemaphoreType.DMA((3,)), pltpu.SemaphoreType.DMA((nt // 2,)),
        ],
        compiler_params=pltpu.CompilerParams(vmem_limit_bytes=56 << 20),
        cost_estimate=pl.CostEstimate(flops=10 * 10**9, bytes_accessed=8 << 20, transcendentals=0),
        name="attention",
    )(ratio, pair, item, image, queries, out_grad, key_values)


CHUNKS = 4
PARTS = CHUNKS // 2
TIMES = ((0, 1), (1, 1), (2.2, 1), (3.3, 1), (5.4, 1), (6.5, 1))
SHARE = (0.5, 0.5, 0.5, 0.5)
MESH = pl.DeviceIdType.MESH
F32 = jnp.float32
BF16 = jnp.bfloat16


def exchange_kernel(kvt, x_own, x1, x2, x3, out_ref,
                    own, core_in, part, z_in, heads, xs, prod, y_out, y_in, final, turned, landed,
                    core_s, core_r, z_s, z_r, right_s, right_r, left_s, left_r,
                    fr_s, fr_r, fl_s, fl_r, y_s, y_r,
                    load_sem, x_sem, xs_s, xs_r, turn_s, turn_r, out_s, out_r):
    dp = lax.axis_index("dp")
    tp = lax.axis_index("tp")
    y = dp // 4
    zh = dp % 4
    x = tp // 4
    zl = tp // 2 % 2
    c = tp % 2
    rows, length = z_in.shape[1:]
    cols = xs.shape[3]
    half = length // 2
    sibling = (dp, x * 4 + zl * 2 + (1 - c))
    across = (dp, x * 4 + (1 - zl) * 2 + c)
    around = [(lax.rem(y + j, 4) * 4 + zh, tp) for j in range(4)]
    beside = [(dp, lax.rem(x + j, 4) * 4 + zl * 2 + c) for j in range(4)]
    right, left = beside[1], beside[3]

    load = pltpu.make_async_copy(kvt.at[c], own, load_sem)
    load.start()
    x_loads = []
    wide = cols // 4

    def piece(j, i):
        return x_own.at[:, pl.ds(pl.multiple_of((4 * i + lax.rem(x + j, 4)) * wide, wide), wide)]

    def place(i):
        return xs.at[x, c, :, pl.ds(i * wide, wide)]

    for i in range(4):
        cp = pltpu.make_async_copy(piece(0, i), place(i), x_sem.at[i])
        cp.start()
        x_loads.append(cp)
    xa = [None]
    for j, src in enumerate((x1, x2, x3)):
        cp = pltpu.make_async_copy(src, xs.at[lax.rem(x + 3 - j, 4), c], x_sem.at[4 + j])
        cp.start()
        xa.append([cp])

    barrier = pltpu.get_barrier_semaphore()
    for partner in (sibling, across, *beside[1:], *around[1:]):
        pl.semaphore_signal(barrier, 1, device_id=partner, device_id_type=MESH)

    def dest(u, h):
        return y * 4 + h, x * 4 + c * 2 + u

    def is_other(d, t):
        return jnp.logical_or(d != dp, t != tp)

    def greet(d, t, n):
        other = is_other(d, t)

        @pl.when(other)
        def _():
            pl.semaphore_signal(barrier, 1, device_id=(d, t), device_id_type=MESH)
        return n + jnp.where(other, 1, 0)

    n = lax.fori_loop(0, 8, lambda i, n: greet(*dest(i % 2, i // 2), n), jnp.int32(8))
    n = lax.fori_loop(0, 8, lambda i, n: greet(y * 4 + i // 2, x * 4 + i % 2 * 2 + zl, n), n)
    pl.semaphore_wait(barrier, n)

    started = []

    def send(src, dst, ss, rs, to):
        cp = pltpu.make_async_remote_copy(src_ref=src, dst_ref=dst, send_sem=ss, recv_sem=rs,
                                          device_id=to, device_id_type=MESH)
        cp.start()
        started.append(cp)
        return cp

    def cut(k):
        return pl.ds(k * rows, rows)

    core = [send(kvt.at[1 - c, :, cut(k)], core_in.at[k], core_s.at[k], core_r.at[k], sibling)
            for k in range(CHUNKS)]
    load.wait()

    zc, rc, lc, frc, flc, yc, tc, xc = ([] for _ in range(8))

    def share(j):
        for cp in xa[j] or x_loads:
            cp.wait()
        here = xs.at[lax.rem(x + 4 - j, 4), c]
        xc.append(send(here, here, xs_s.at[j], xs_r.at[j], sibling))

    def reduce_core(k):
        core[k].wait_recv()
        part[k] = (own[1 - zl, cut(k)].astype(F32) + core_in[k, 1 - zl].astype(F32)).astype(BF16)
        zc.append(send(part.at[k], z_in.at[k], z_s.at[k], z_r.at[k], across))

    def reduce_z(k):
        zc[k].wait_recv()
        heads[k, x] = (own[zl, cut(k)].astype(F32) + core_in[k, zl].astype(F32) + z_in[k].astype(F32)).astype(BF16)
        here = heads.at[k, x]
        rc.append(send(here, here, right_s.at[k], right_r.at[k], right))
        lc.append(send(here, here, left_s.at[k], left_r.at[k], left))

    def forward(k):
        rc[k].wait_recv()
        a = heads.at[k, lax.rem(x + 3, 4), :, pl.ds(0, half)]
        frc.append(send(a, a, fr_s.at[k], fr_r.at[k], right))
        lc[k].wait_recv()
        b = heads.at[k, lax.rem(x + 1, 4), :, pl.ds(half, half)]
        flc.append(send(b, b, fl_s.at[k], fl_r.at[k], left))

    def multiply(k):
        frc[k].wait_recv()
        flc[k].wait_recv()
        if k == 0:
            for cp in xc:
                cp.wait_recv()
        lhs = heads[k].reshape(4 * rows, length)
        res = jnp.dot(lhs, xs[...].reshape(length, cols), preferred_element_type=F32)
        for q in range(4):
            prod[k, q] = res[:, q * wide:(q + 1) * wide]
        sent = []
        for j in (2, 1, 3):
            y_out[k, j - 1] = prod[k, lax.rem(y + j, 4)].astype(BF16)
            sent.append(send(y_out.at[k, j - 1], y_in.at[k, j - 1], y_s.at[k, j - 1], y_r.at[k, j - 1], around[j]))
        yc.append(sent)

    spot = zh * 2 + zl

    def out_copy(k, q):
        d, t = dest(k // PARTS, lax.rem(x + 4 - q, 4))
        return d, t, pltpu.make_async_remote_copy(
            src_ref=turned.at[k, q], dst_ref=landed.at[spot, k % PARTS], send_sem=out_s.at[k * 4 + q],
            recv_sem=out_r.at[spot, k % PARTS], device_id=(d, t), device_id_type=MESH)

    def deliver(k):
        for cp in yc[k]:
            cp.wait_recv()
        total = (prod[k, y] + y_in[k, 0].astype(F32) + y_in[k, 1].astype(F32) + y_in[k, 2].astype(F32)).astype(BF16)
        for h in range(4):
            final[k, h] = total[h * rows:(h + 1) * rows]
        turned[k, 0] = final[k, x]
        tc.append([send(final.at[k, lax.rem(x + j, 4)], turned.at[k, j], turn_s.at[k, j - 1], turn_r.at[k, j - 1],
                        beside[j]) for j in (2, 1, 3)])

    def scatter(k):
        for cp in tc[k]:
            cp.wait_recv()

        def one(q, carry):
            d, t, cp = out_copy(k, q)
            other = is_other(d, t)

            @pl.when(other)
            def _():
                cp.start()

            @pl.when(jnp.logical_not(other))
            def _():
                pltpu.make_async_copy(turned.at[k, q], landed.at[spot, k % PARTS], out_r.at[spot, k % PARTS]).start()
            return carry
        lax.fori_loop(0, 4, one, 0)

    stages = (reduce_core, reduce_z, forward, multiply, deliver, scatter)
    order = sorted((start + k * gap, i, k) for i, (start, gap) in enumerate(TIMES) for k in range(CHUNKS))
    order = sorted(order + [(SHARE[j], -1, j) for j in range(4)])
    for _, i, k in order:
        share(k) if i < 0 else stages[i](k)

    def collect(i, total):
        new = []
        for p in range(PARTS):
            pltpu.make_async_copy(landed.at[i, p], landed.at[i, p], out_r.at[i, p]).wait()
            new.append(total[p] + landed[i, p].astype(F32))
        return tuple(new)

    zero = jnp.zeros((rows, cols // 4), F32)
    sums = lax.fori_loop(0, 8, collect, (zero,) * PARTS)
    for p in range(PARTS):
        out_ref[p * rows:(p + 1) * rows] = sums[p]

    for cp in started:
        cp.wait_send()

    def drain(j, carry):
        d, t, cp = out_copy(j // 4, j % 4)

        @pl.when(is_other(d, t))
        def _():
            cp.wait_send()
        return carry
    lax.fori_loop(0, 4 * CHUNKS, drain, 0)


def exchange(kvt, x_own, others):
    length = kvt.shape[3]
    cols = x_own.shape[1] // 4
    rows = HD // CHUNKS
    sem = pltpu.SemaphoreType.DMA
    n = CHUNKS
    return pl.pallas_call(
        exchange_kernel,
        out_shape=jax.ShapeDtypeStruct((PARTS * rows, cols // 4), F32),
        in_specs=[pl.BlockSpec(memory_space=pl.ANY)] * 5,
        out_specs=pl.BlockSpec(memory_space=pltpu.VMEM),
        scratch_shapes=[
            pltpu.VMEM((2, HD, length), BF16), pltpu.VMEM((n, 2, rows, length), BF16),
            pltpu.VMEM((n, rows, length), BF16), pltpu.VMEM((n, rows, length), BF16),
            pltpu.VMEM((n, 4, rows, length), BF16), pltpu.VMEM((4, 2, TILE, cols), BF16),
            pltpu.VMEM((n, 4, 4 * rows, cols // 4), F32),
            pltpu.VMEM((n, 3, 4 * rows, cols // 4), BF16), pltpu.VMEM((n, 3, 4 * rows, cols // 4), BF16),
            pltpu.VMEM((n, 4, rows, cols // 4), BF16), pltpu.VMEM((n, 4, rows, cols // 4), BF16),
            pltpu.VMEM((8, PARTS, rows, cols // 4), BF16),
        ] + [sem((n,))] * 12 + [sem((n, 3))] * 2 + [sem, sem((7,)), sem((4,)), sem((4,)),
                                                    sem((n, 3)), sem((n, 3)), sem((4 * n,)), sem((8, PARTS))],
        compiler_params=pltpu.CompilerParams(collective_id=0, has_side_effects=True, vmem_limit_bytes=56 << 20),
        cost_estimate=pl.CostEstimate(flops=10**9, bytes_accessed=8 << 20, transcendentals=0),
        name="exchange",
    )(kvt, x_own, *others)


def local(input_rows, queries, key_values, out_grad, item_logratio, pair_ids, tile_item, tile_image):
    t = lax.axis_index("tp")
    rows = input_rows[0]
    split = rows.reshape(rows.shape[0], 4, 4, -1)
    others = []
    for dx in range(1, 4):
        to = (t // 4 + dx) % 4
        pairs = [(a, (a + 4 * dx) % 16) for a in range(16)]
        others.append(lax.ppermute(lax.dynamic_index_in_dim(split, to, 2, False).reshape(rows.shape[0], -1), "tp", pairs))
    dq, kvt = attention(queries, out_grad, key_values, item_logratio, pair_ids, tile_item, tile_image)
    return dq, exchange(kvt, rows, others).T


def solution(mesh):
    in_specs = (P("dp", "tp", None), P("dp", None, "tp"), P("dp", None, None), P("dp", None, "tp"),
                P("dp", None), P("dp", None), P("dp", None), P("dp", None))
    out_specs = (P("dp", None, "tp"), P("dp", "tp"))
    return jax.shard_map(local, mesh=mesh, in_specs=in_specs, out_specs=out_specs, check_vma=False)
```

```python
import functools, math
import jax, jax.numpy as jnp
from jax import lax
from jax.experimental import pallas as pl
from jax.experimental.pallas import tpu as pltpu

from jax.sharding import PartitionSpec as P

KVH = 4; HD = 128; TILE = 128; BETA = 0.1
MASKED = -1e30
LOG2E = 1.4426950408889634

def attention_kernel(ratio_h, pair_h, item_h, image_h, q_hbm, og_hbm, kv_hbm, dq_hbm, kvt_ref,
                     kv, q_ref, og_ref, dq_ref, s0, s1, dp0, dp1, acc, ratio, pair, item, image,
                     lo_s, hi_s, n_s, order, work, z_s, small_sem, big_sem, dq_sem):
    group = lax.axis_size("tp") // KVH
    g = lax.axis_index("tp") // group
    nt = item.shape[1]
    items = ratio.shape[1]
    small = [pltpu.make_async_copy(a, b, small_sem.at[i])
             for i, (a, b) in enumerate(((ratio_h, ratio), (pair_h, pair), (item_h, item), (image_h, image)))]
    for cp in small:
        cp.start()
    big = [pltpu.make_async_copy(kv_hbm.at[0, :, pl.ds(pl.multiple_of(g * 2 * HD, 2 * HD), 2 * HD)], kv, big_sem.at[0]),
           pltpu.make_async_copy(q_hbm.at[0], q_ref, big_sem.at[1]),
           pltpu.make_async_copy(og_hbm.at[0], og_ref, big_sem.at[2])]
    for cp in big:
        cp.start()
    inv_root = 1.0 / math.sqrt(HD)
    c2 = inv_root * LOG2E
    W = 2 * TILE
    acc[...] = jnp.zeros_like(acc)
    for cp in small:
        cp.wait()
    lo_s[0] = 0
    for i in range(1, nt):
        lo_s[i] = jnp.where(item[0, i] == item[0, i - 1], lo_s[i - 1], i)
    hi_s[nt - 1] = nt - 1
    for i in reversed(range(nt - 1)):
        same = (image[0, i] > 0) & (image[0, i] == image[0, i + 1]) & (item[0, i] == item[0, i + 1])
        hi_s[i] = jnp.where(same, hi_s[i + 1], i)
    for a in range(items):
        other = jnp.float32(0.0)
        p = jnp.float32(1.0)
        for b in range(items):
            if b != a:
                same = pair[0, a] == pair[0, b]
                other = other + jnp.where(same, ratio[0, b], 0.0)
                if a < b:
                    p = jnp.where(same, -1.0, p)
        z_s[a] = BETA * p * (other - ratio[0, a])
        z_s[items + a] = p

    for i in range(nt):
        n_s[i] = (hi_s[i] - lo_s[i] + 2) // 2

    def place(t, pos):
        i = lax.rem(t, nt)
        order[pos] = i
        return pos + jnp.where(n_s[i] == nt // 2 - t // nt, 1, 0)

    lax.fori_loop(0, nt * nt // 2, place, jnp.int32(0))

    def match(t, carry):
        i, w = carry
        a = order[jnp.minimum(i, nt - 1)]
        b = order[jnp.minimum(i + 1, nt - 1)]
        both = (i + 1 < nt) & (n_s[a] - n_s[b] <= 1)
        more = i < nt
        work[3 * w] = a
        work[3 * w + 1] = jnp.where(both, b, a)
        work[3 * w + 2] = jnp.where(both, 1, 0)
        return i + jnp.where(both, 2, 1), w + jnp.where(more, 1, 0)

    _, count = lax.fori_loop(0, nt, match, (jnp.int32(0), jnp.int32(0)))
    for cp in big:
        cp.wait()

    def block(I, real, n, spare, s_scr, dp_scr):
        lo = lo_s[I]
        hi = hi_s[I]
        img = image[0, I]
        it = item[0, I]
        r0 = pl.multiple_of(I * TILE, TILE)
        st = pl.multiple_of(jnp.clip(hi + 1 - 2 * n, 0, nt - 2 * n) * TILE, TILE)
        first = lo * TILE - st
        v = {}

        def stage1():
            qi = q_ref[pl.ds(r0, TILE), :]
            q2 = jnp.concatenate([qi[:, :HD], qi[:, HD:]], axis=0)
            coef = z_s[items + it] * real.astype(jnp.float32) / (1.0 + jnp.exp(jnp.full((8, HD), z_s[it], jnp.float32)))
            coef = jnp.concatenate([coef[:1], coef[:1]], axis=1)
            wi = (og_ref[pl.ds(r0, TILE), :].astype(jnp.float32) * coef).astype(jnp.bfloat16)
            w2 = jnp.concatenate([wi[:, :HD], wi[:, HD:]], axis=0)
            v["q2t"] = q2.T
            v["w2t"] = w2.T
            row = lax.broadcasted_iota(jnp.int32, (TILE, 1), 0)
            row = jnp.concatenate([row, row], axis=0)
            last = jnp.where(img > 0, jnp.full((2 * TILE, 1), (hi + 1) * TILE - 1 - st), r0 - st + row)
            m = None
            for ch in range(n):
                rows = pl.ds(st + ch * W, W)
                s = lax.dot_general(q2, kv[rows, :HD], (((1,), (1,)), ((), ())), preferred_element_type=jnp.float32)
                if ch <= spare or ch >= n - 2:
                    col = lax.broadcasted_iota(jnp.int32, (1, W), 1) + ch * W
                    ok = (col <= last) & (col >= first)
                    s = jnp.where(ok, s, MASKED)
                s_scr[:, ch * W:(ch + 1) * W] = s
                mm = jnp.maximum(s[:, :HD], s[:, HD:])
                m = mm if m is None else jnp.maximum(m, mm)
                dp_scr[:, ch * W:(ch + 1) * W] = lax.dot_general(
                    w2, kv[rows, HD:], (((1,), (1,)), ((), ())), preferred_element_type=jnp.float32)
            v["m"] = jnp.max(m, axis=1, keepdims=True) * c2

        def stage2():
            mr = v["m"]
            l = r = None
            for ch in range(n):
                cols = slice(ch * W, (ch + 1) * W)
                p = jnp.exp2(s_scr[:, cols] * c2 - mr)
                s_scr[:, cols] = p
                pd = p * dp_scr[:, cols]
                ll = p[:, :HD] + p[:, HD:]
                rr = pd[:, :HD] + pd[:, HD:]
                l = ll if l is None else l + ll
                r = rr if r is None else r + rr
            v["inv"] = 1.0 / jnp.sum(l, axis=1, keepdims=True)
            v["rd"] = jnp.sum(r, axis=1, keepdims=True) * v["inv"]

        def stage3():
            inv, rd = v["inv"], v["rd"]
            dq = None
            for ch in range(n):
                rows = pl.ds(st + ch * W, W)
                cols = slice(ch * W, (ch + 1) * W)
                at = s_scr[:, cols] * inv
                ds = (at * (dp_scr[:, cols] - rd)).astype(jnp.bfloat16)
                at = at.astype(jnp.bfloat16)
                d = jnp.dot(ds, kv[rows, :HD], preferred_element_type=jnp.float32)
                dq = d if dq is None else dq + d
                acc[:HD, rows] += jnp.dot(v["q2t"], ds, preferred_element_type=jnp.float32)
                acc[HD:, rows] += jnp.dot(v["w2t"], at, preferred_element_type=jnp.float32)
            dq = (dq * inv_root).astype(jnp.bfloat16)
            to = pl.ds(pl.multiple_of(jnp.where(real > 0, I, nt) * TILE, TILE), TILE)
            dq_ref[to, :HD] = dq[:TILE]
            dq_ref[to, HD:] = dq[TILE:]

        return stage1, stage2, stage3

    def out_copy(i):
        here = pl.ds(pl.multiple_of(i * TILE, TILE), TILE)
        return pltpu.make_async_copy(dq_ref.at[here], dq_hbm.at[0, here], dq_sem.at[i])

    def row_pair(j, carry):
        a, b, real = work[3 * j], work[3 * j + 1], work[3 * j + 2]
        n_here = n_s[a]
        for n in range(1, nt // 2 + 1):
            @pl.when(n_here == n)
            def _():
                one = block(a, jnp.int32(1), n, 1, s0, dp0)
                two = block(b, real, n, 1, s1, dp1)
                for f, g2 in zip(one, two):
                    f()
                    g2()
        out_copy(a).start()

        @pl.when(real > 0)
        def _():
            out_copy(b).start()
        return carry

    lax.fori_loop(0, count, row_pair, 0)
    for i in range(nt // 4):
        for z in range(2):
            frm = slice((2 * i + z) * W, (2 * i + z + 1) * W)
            to = slice(i * W, (i + 1) * W)
            kvt_ref[0, z, :, to] = (acc[:HD, frm] * inv_root).astype(jnp.bfloat16)
            kvt_ref[1, z, :, to] = acc[HD:, frm].astype(jnp.bfloat16)

    def finish(i, carry):
        out_copy(i).wait()
        return carry
    lax.fori_loop(0, nt, finish, 0)


def attention(queries, out_grad, key_values, ratio, pair, item, image):
    L = queries.shape[1]
    nt = L // TILE
    hbm = pl.BlockSpec(memory_space=pl.ANY)
    wide = pltpu.VMEM((2 * TILE, L), jnp.float32)
    low = pltpu.VMEM((L, 2 * HD), jnp.bfloat16)
    return pl.pallas_call(
        attention_kernel,
        out_shape=[jax.ShapeDtypeStruct(queries.shape, jnp.bfloat16),
                   jax.ShapeDtypeStruct((2, 2, HD, L // 2), jnp.bfloat16)],
        in_specs=[hbm] * 7,
        out_specs=[hbm, pl.BlockSpec(memory_space=pltpu.VMEM)],
        scratch_shapes=[low, low, low, pltpu.VMEM((L + TILE, 2 * HD), jnp.bfloat16), wide, wide, wide, wide,
            pltpu.VMEM((2 * HD, L), jnp.float32),
            pltpu.SMEM(ratio.shape, jnp.float32),
            pltpu.SMEM(pair.shape, jnp.int32),
            pltpu.SMEM(item.shape, jnp.int32),
            pltpu.SMEM(image.shape, jnp.int32),
            pltpu.SMEM((nt,), jnp.int32),
            pltpu.SMEM((nt,), jnp.int32),
            pltpu.SMEM((nt,), jnp.int32),
            pltpu.SMEM((nt + 1,), jnp.int32),
            pltpu.SMEM((3 * (nt + 1),), jnp.int32),
            pltpu.SMEM((2 * ratio.shape[1],), jnp.float32),
            pltpu.SemaphoreType.DMA((4,)), pltpu.SemaphoreType.DMA((3,)), pltpu.SemaphoreType.DMA((nt,)),
        ],
        compiler_params=pltpu.CompilerParams(vmem_limit_bytes=56 << 20),
        cost_estimate=pl.CostEstimate(flops=10 * 10**9, bytes_accessed=8 << 20, transcendentals=0),
        name="attention",
    )(ratio, pair, item, image, queries, out_grad, key_values)


CHUNKS = 4
PARTS = CHUNKS // 2
TIMES = ((0, 1), (1, 1), (2.2, 1), (3.3, 1), (5.4, 1), (6.5, 1))
SHARE = (0.5, 0.5, 0.5, 0.5)
MESH = pl.DeviceIdType.MESH
F32 = jnp.float32
BF16 = jnp.bfloat16


def exchange_kernel(kvt, x_own, x1, x2, x3, out_ref,
                    own, core_in, part, z_in, heads, xs, prod, y_out, y_in, final, turned, landed,
                    core_s, core_r, z_s, z_r, right_s, right_r, left_s, left_r,
                    fr_s, fr_r, fl_s, fl_r, y_s, y_r,
                    load_sem, x_sem, xs_s, xs_r, turn_s, turn_r, out_s, out_r):
    dp = lax.axis_index("dp")
    tp = lax.axis_index("tp")
    y = dp // 4
    zh = dp % 4
    x = tp // 4
    zl = tp // 2 % 2
    c = tp % 2
    rows, length = z_in.shape[1:]
    cols = xs.shape[3]
    half = length // 2
    sibling = (dp, x * 4 + zl * 2 + (1 - c))
    across = (dp, x * 4 + (1 - zl) * 2 + c)
    around = [(lax.rem(y + j, 4) * 4 + zh, tp) for j in range(4)]
    beside = [(dp, lax.rem(x + j, 4) * 4 + zl * 2 + c) for j in range(4)]
    right, left = beside[1], beside[3]

    load = pltpu.make_async_copy(kvt.at[c], own, load_sem)
    load.start()
    x_loads = []
    wide = cols // 4

    def piece(j, i):
        return x_own.at[:, pl.ds(pl.multiple_of((4 * i + lax.rem(x + j, 4)) * wide, wide), wide)]

    def place(i):
        return xs.at[x, c, :, pl.ds(i * wide, wide)]

    for i in range(4):
        cp = pltpu.make_async_copy(piece(0, i), place(i), x_sem.at[i])
        cp.start()
        x_loads.append(cp)
    xa = [None]
    for j, src in enumerate((x1, x2, x3)):
        cp = pltpu.make_async_copy(src, xs.at[lax.rem(x + 3 - j, 4), c], x_sem.at[4 + j])
        cp.start()
        xa.append([cp])

    barrier = pltpu.get_barrier_semaphore()
    for partner in (sibling, across, *beside[1:], *around[1:]):
        pl.semaphore_signal(barrier, 1, device_id=partner, device_id_type=MESH)

    def dest(u, h):
        return y * 4 + h, x * 4 + c * 2 + u

    def is_other(d, t):
        return jnp.logical_or(d != dp, t != tp)

    def greet(d, t, n):
        other = is_other(d, t)

        @pl.when(other)
        def _():
            pl.semaphore_signal(barrier, 1, device_id=(d, t), device_id_type=MESH)
        return n + jnp.where(other, 1, 0)

    n = lax.fori_loop(0, 8, lambda i, n: greet(*dest(i % 2, i // 2), n), jnp.int32(8))
    n = lax.fori_loop(0, 8, lambda i, n: greet(y * 4 + i // 2, x * 4 + i % 2 * 2 + zl, n), n)
    pl.semaphore_wait(barrier, n)

    started = []

    def send(src, dst, ss, rs, to):
        cp = pltpu.make_async_remote_copy(src_ref=src, dst_ref=dst, send_sem=ss, recv_sem=rs,
                                          device_id=to, device_id_type=MESH)
        cp.start()
        started.append(cp)
        return cp

    def cut(k):
        return pl.ds(k * rows, rows)

    core = [send(kvt.at[1 - c, :, cut(k)], core_in.at[k], core_s.at[k], core_r.at[k], sibling)
            for k in range(CHUNKS)]
    load.wait()

    zc, rc, lc, frc, flc, yc, tc, xc = ([] for _ in range(8))

    def share(j):
        for cp in xa[j] or x_loads:
            cp.wait()
        here = xs.at[lax.rem(x + 4 - j, 4), c]
        xc.append(send(here, here, xs_s.at[j], xs_r.at[j], sibling))

    def reduce_core(k):
        core[k].wait_recv()
        part[k] = (own[1 - zl, cut(k)].astype(F32) + core_in[k, 1 - zl].astype(F32)).astype(BF16)
        zc.append(send(part.at[k], z_in.at[k], z_s.at[k], z_r.at[k], across))

    def reduce_z(k):
        zc[k].wait_recv()
        heads[k, x] = (own[zl, cut(k)].astype(F32) + core_in[k, zl].astype(F32) + z_in[k].astype(F32)).astype(BF16)
        here = heads.at[k, x]
        rc.append(send(here, here, right_s.at[k], right_r.at[k], right))
        lc.append(send(here, here, left_s.at[k], left_r.at[k], left))

    def forward(k):
        rc[k].wait_recv()
        a = heads.at[k, lax.rem(x + 3, 4), :, pl.ds(0, half)]
        frc.append(send(a, a, fr_s.at[k], fr_r.at[k], right))
        lc[k].wait_recv()
        b = heads.at[k, lax.rem(x + 1, 4), :, pl.ds(half, half)]
        flc.append(send(b, b, fl_s.at[k], fl_r.at[k], left))

    def multiply(k):
        frc[k].wait_recv()
        flc[k].wait_recv()
        if k == 0:
            for cp in xc:
                cp.wait_recv()
        lhs = heads[k].reshape(4 * rows, length)
        res = jnp.dot(lhs, xs[...].reshape(length, cols), preferred_element_type=F32)
        for q in range(4):
            prod[k, q] = res[:, q * wide:(q + 1) * wide]
        sent = []
        for j in (2, 1, 3):
            y_out[k, j - 1] = prod[k, lax.rem(y + j, 4)].astype(BF16)
            sent.append(send(y_out.at[k, j - 1], y_in.at[k, j - 1], y_s.at[k, j - 1], y_r.at[k, j - 1], around[j]))
        yc.append(sent)

    spot = zh * 2 + zl

    def out_copy(k, q):
        d, t = dest(k // PARTS, lax.rem(x + 4 - q, 4))
        return d, t, pltpu.make_async_remote_copy(
            src_ref=turned.at[k, q], dst_ref=landed.at[spot, k % PARTS], send_sem=out_s.at[k * 4 + q],
            recv_sem=out_r.at[spot, k % PARTS], device_id=(d, t), device_id_type=MESH)

    def deliver(k):
        for cp in yc[k]:
            cp.wait_recv()
        total = (prod[k, y] + y_in[k, 0].astype(F32) + y_in[k, 1].astype(F32) + y_in[k, 2].astype(F32)).astype(BF16)
        for h in range(4):
            final[k, h] = total[h * rows:(h + 1) * rows]
        turned[k, 0] = final[k, x]
        tc.append([send(final.at[k, lax.rem(x + j, 4)], turned.at[k, j], turn_s.at[k, j - 1], turn_r.at[k, j - 1],
                        beside[j]) for j in (2, 1, 3)])

    def scatter(k):
        for cp in tc[k]:
            cp.wait_recv()

        def one(q, carry):
            d, t, cp = out_copy(k, q)
            other = is_other(d, t)

            @pl.when(other)
            def _():
                cp.start()

            @pl.when(jnp.logical_not(other))
            def _():
                pltpu.make_async_copy(turned.at[k, q], landed.at[spot, k % PARTS], out_r.at[spot, k % PARTS]).start()
            return carry
        lax.fori_loop(0, 4, one, 0)

    stages = (reduce_core, reduce_z, forward, multiply, deliver, scatter)
    order = sorted((start + k * gap, i, k) for i, (start, gap) in enumerate(TIMES) for k in range(CHUNKS))
    order = sorted(order + [(SHARE[j], -1, j) for j in range(4)])
    for _, i, k in order:
        share(k) if i < 0 else stages[i](k)

    def collect(i, total):
        new = []
        for p in range(PARTS):
            pltpu.make_async_copy(landed.at[i, p], landed.at[i, p], out_r.at[i, p]).wait()
            new.append(total[p] + landed[i, p].astype(F32))
        return tuple(new)

    zero = jnp.zeros((rows, cols // 4), F32)
    sums = lax.fori_loop(0, 8, collect, (zero,) * PARTS)
    for p in range(PARTS):
        out_ref[p * rows:(p + 1) * rows] = sums[p]

    for cp in started:
        cp.wait_send()

    def drain(j, carry):
        d, t, cp = out_copy(j // 4, j % 4)

        @pl.when(is_other(d, t))
        def _():
            cp.wait_send()
        return carry
    lax.fori_loop(0, 4 * CHUNKS, drain, 0)


def exchange(kvt, x_own, others):
    length = kvt.shape[3]
    cols = x_own.shape[1] // 4
    rows = HD // CHUNKS
    sem = pltpu.SemaphoreType.DMA
    n = CHUNKS
    return pl.pallas_call(
        exchange_kernel,
        out_shape=jax.ShapeDtypeStruct((PARTS * rows, cols // 4), F32),
        in_specs=[pl.BlockSpec(memory_space=pl.ANY)] * 5,
        out_specs=pl.BlockSpec(memory_space=pltpu.VMEM),
        scratch_shapes=[
            pltpu.VMEM((2, HD, length), BF16), pltpu.VMEM((n, 2, rows, length), BF16),
            pltpu.VMEM((n, rows, length), BF16), pltpu.VMEM((n, rows, length), BF16),
            pltpu.VMEM((n, 4, rows, length), BF16), pltpu.VMEM((4, 2, TILE, cols), BF16),
            pltpu.VMEM((n, 4, 4 * rows, cols // 4), F32),
            pltpu.VMEM((n, 3, 4 * rows, cols // 4), BF16), pltpu.VMEM((n, 3, 4 * rows, cols // 4), BF16),
            pltpu.VMEM((n, 4, rows, cols // 4), BF16), pltpu.VMEM((n, 4, rows, cols // 4), BF16),
            pltpu.VMEM((8, PARTS, rows, cols // 4), BF16),
        ] + [sem((n,))] * 12 + [sem((n, 3))] * 2 + [sem, sem((7,)), sem((4,)), sem((4,)),
                                                    sem((n, 3)), sem((n, 3)), sem((4 * n,)), sem((8, PARTS))],
        compiler_params=pltpu.CompilerParams(collective_id=0, has_side_effects=True, vmem_limit_bytes=56 << 20),
        cost_estimate=pl.CostEstimate(flops=10**9, bytes_accessed=8 << 20, transcendentals=0),
        name="exchange",
    )(kvt, x_own, *others)


def deal_kernel(x_in, *rest):
    outs, sem = rest[:3], rest[3]
    x = lax.axis_index("tp") // 4
    wide = outs[0].shape[1] // 4
    copies = []
    for j in range(1, 4):
        for i in range(4):
            src = x_in.at[:, pl.ds(pl.multiple_of((4 * i + lax.rem(x + j, 4)) * wide, wide), wide)]
            copies.append(pltpu.make_async_copy(src, outs[j - 1].at[:, pl.ds(i * wide, wide)], sem.at[j - 1, i]))
    for cp in copies:
        cp.start()
    for cp in copies:
        cp.wait()


def deal(rows):
    hbm = pl.BlockSpec(memory_space=pl.ANY)
    shape = jax.ShapeDtypeStruct((rows.shape[0], rows.shape[1] // 4), BF16)
    return pl.pallas_call(
        deal_kernel, out_shape=[shape] * 3, in_specs=[hbm], out_specs=[hbm] * 3,
        scratch_shapes=[pltpu.SemaphoreType.DMA((3, 4))], name="deal",
    )(rows)


def local(input_rows, queries, key_values, out_grad, item_logratio, pair_ids, tile_item, tile_image):
    rows = input_rows[0]
    others = []
    for dx, block in zip(range(1, 4), deal(rows)):
        others.append(lax.ppermute(block, "tp", [(a, (a + 4 * dx) % 16) for a in range(16)]))
    dq, kvt = attention(queries, out_grad, key_values, item_logratio, pair_ids, tile_item, tile_image)
    return dq, exchange(kvt, rows, others).T


def solution(mesh):
    in_specs = (P("dp", "tp", None), P("dp", None, "tp"), P("dp", None, None), P("dp", None, "tp"),
                P("dp", None), P("dp", None), P("dp", None), P("dp", None))
    out_specs = (P("dp", None, "tp"), P("dp", "tp"))
    return jax.shard_map(local, mesh=mesh, in_specs=in_specs, out_specs=out_specs, check_vma=False)
```

```python
import functools, math
import jax, jax.numpy as jnp
from jax import lax
from jax.experimental import pallas as pl
from jax.experimental.pallas import tpu as pltpu

from jax.sharding import PartitionSpec as P

KVH = 4; HD = 128; TILE = 128; BETA = 0.1
MASKED = -1e30
LOG2E = 1.4426950408889634

def attention_kernel(ratio_h, pair_h, item_h, image_h, q_hbm, og_hbm, kv_hbm, dq_hbm, kvt_ref,
                     kv, q_ref, og_ref, dq_ref, s0, s1, dp0, dp1, acc, ratio, pair, item, image,
                     lo_s, hi_s, n_s, order, work, z_s, small_sem, big_sem, dq_sem):
    group = lax.axis_size("tp") // KVH
    g = lax.axis_index("tp") // group
    nt = item.shape[1]
    items = ratio.shape[1]
    small = [pltpu.make_async_copy(a, b, small_sem.at[i])
             for i, (a, b) in enumerate(((ratio_h, ratio), (pair_h, pair), (item_h, item), (image_h, image)))]
    for cp in small:
        cp.start()
    big = [pltpu.make_async_copy(kv_hbm.at[0, :, pl.ds(pl.multiple_of(g * 2 * HD, 2 * HD), 2 * HD)], kv, big_sem.at[0]),
           pltpu.make_async_copy(q_hbm.at[0], q_ref, big_sem.at[1]),
           pltpu.make_async_copy(og_hbm.at[0], og_ref, big_sem.at[2])]
    for cp in big:
        cp.start()
    inv_root = 1.0 / math.sqrt(HD)
    c2 = inv_root * LOG2E
    W = 2 * TILE
    acc[...] = jnp.zeros_like(acc)
    for cp in small:
        cp.wait()
    lo_s[0] = 0
    for i in range(1, nt):
        lo_s[i] = jnp.where(item[0, i] == item[0, i - 1], lo_s[i - 1], i)
    hi_s[nt - 1] = nt - 1
    for i in reversed(range(nt - 1)):
        same = (image[0, i] > 0) & (image[0, i] == image[0, i + 1]) & (item[0, i] == item[0, i + 1])
        hi_s[i] = jnp.where(same, hi_s[i + 1], i)
    for a in range(items):
        other = jnp.float32(0.0)
        p = jnp.float32(1.0)
        for b in range(items):
            if b != a:
                same = pair[0, a] == pair[0, b]
                other = other + jnp.where(same, ratio[0, b], 0.0)
                if a < b:
                    p = jnp.where(same, -1.0, p)
        z_s[a] = BETA * p * (other - ratio[0, a])
        z_s[items + a] = p

    for i in range(nt):
        n_s[i] = (hi_s[i] - lo_s[i] + 2) // 2

    def place(t, pos):
        i = lax.rem(t, nt)
        order[pos] = i
        return pos + jnp.where(n_s[i] == nt // 2 - t // nt, 1, 0)

    lax.fori_loop(0, nt * nt // 2, place, jnp.int32(0))

    def match(t, carry):
        i, w = carry
        a = order[jnp.minimum(i, nt - 1)]
        b = order[jnp.minimum(i + 1, nt - 1)]
        both = (i + 1 < nt) & (n_s[a] - n_s[b] <= 1)
        more = i < nt
        work[3 * w] = a
        work[3 * w + 1] = jnp.where(both, b, a)
        work[3 * w + 2] = jnp.where(both, 1, 0)
        return i + jnp.where(both, 2, 1), w + jnp.where(more, 1, 0)

    _, count = lax.fori_loop(0, nt, match, (jnp.int32(0), jnp.int32(0)))
    for cp in big:
        cp.wait()

    def block(I, real, n, spare, s_scr, dp_scr):
        lo = lo_s[I]
        hi = hi_s[I]
        img = image[0, I]
        it = item[0, I]
        r0 = pl.multiple_of(I * TILE, TILE)
        st = pl.multiple_of(jnp.clip(hi + 1 - 2 * n, 0, nt - 2 * n) * TILE, TILE)
        first = lo * TILE - st
        v = {}

        def stage1():
            qi = q_ref[pl.ds(r0, TILE), :]
            q2 = jnp.concatenate([qi[:, :HD], qi[:, HD:]], axis=0)
            coef = z_s[items + it] * real.astype(jnp.float32) / (1.0 + jnp.exp(jnp.full((8, HD), z_s[it], jnp.float32)))
            coef = jnp.concatenate([coef[:1], coef[:1]], axis=1)
            wi = (og_ref[pl.ds(r0, TILE), :].astype(jnp.float32) * coef).astype(jnp.bfloat16)
            w2 = jnp.concatenate([wi[:, :HD], wi[:, HD:]], axis=0)
            v["q2t"] = q2.T
            v["w2t"] = w2.T
            row = lax.broadcasted_iota(jnp.int32, (TILE, 1), 0)
            row = jnp.concatenate([row, row], axis=0)
            last = jnp.where(img > 0, jnp.full((2 * TILE, 1), (hi + 1) * TILE - 1 - st), r0 - st + row)
            m = None
            for ch in range(n):
                rows = pl.ds(st + ch * W, W)
                s = lax.dot_general(q2, kv[rows, :HD], (((1,), (1,)), ((), ())), preferred_element_type=jnp.float32)
                if ch <= spare or ch >= n - 2:
                    col = lax.broadcasted_iota(jnp.int32, (1, W), 1) + ch * W
                    ok = (col <= last) & (col >= first)
                    s = jnp.where(ok, s, MASKED)
                s_scr[:, ch * W:(ch + 1) * W] = s
                mm = jnp.maximum(s[:, :HD], s[:, HD:])
                m = mm if m is None else jnp.maximum(m, mm)
                dp_scr[:, ch * W:(ch + 1) * W] = lax.dot_general(
                    w2, kv[rows, HD:], (((1,), (1,)), ((), ())), preferred_element_type=jnp.float32)
            v["m"] = jnp.max(m, axis=1, keepdims=True) * c2

        def stage2():
            mr = v["m"]
            l = r = None
            for ch in range(n):
                cols = slice(ch * W, (ch + 1) * W)
                p = jnp.exp2(s_scr[:, cols] * c2 - mr)
                s_scr[:, cols] = p
                pd = p * dp_scr[:, cols]
                ll = p[:, :HD] + p[:, HD:]
                rr = pd[:, :HD] + pd[:, HD:]
                l = ll if l is None else l + ll
                r = rr if r is None else r + rr
            v["inv"] = 1.0 / jnp.sum(l, axis=1, keepdims=True)
            v["rd"] = jnp.sum(r, axis=1, keepdims=True) * v["inv"]

        def stage3():
            inv, rd = v["inv"], v["rd"]
            dq = None
            for ch in range(n):
                rows = pl.ds(st + ch * W, W)
                cols = slice(ch * W, (ch + 1) * W)
                at = s_scr[:, cols] * inv
                ds = (at * (dp_scr[:, cols] - rd)).astype(jnp.bfloat16)
                at = at.astype(jnp.bfloat16)
                d = jnp.dot(ds, kv[rows, :HD], preferred_element_type=jnp.float32)
                dq = d if dq is None else dq + d
                acc[:HD, rows] += jnp.dot(v["q2t"], ds, preferred_element_type=jnp.float32)
                acc[HD:, rows] += jnp.dot(v["w2t"], at, preferred_element_type=jnp.float32)
            dq = (dq * inv_root).astype(jnp.bfloat16)
            to = pl.ds(pl.multiple_of(jnp.where(real > 0, I, nt) * TILE, TILE), TILE)
            dq_ref[to, :HD] = dq[:TILE]
            dq_ref[to, HD:] = dq[TILE:]

        return stage1, stage2, stage3

    def out_copy(i):
        here = pl.ds(pl.multiple_of(i * TILE, TILE), TILE)
        return pltpu.make_async_copy(dq_ref.at[here], dq_hbm.at[0, here], dq_sem.at[i])

    def row_pair(j, carry):
        a, b, real = work[3 * j], work[3 * j + 1], work[3 * j + 2]
        n_here = n_s[a]
        for n in range(1, nt // 2 + 1):
            @pl.when(n_here == n)
            def _():
                one = block(a, jnp.int32(1), n, 1, s0, dp0)
                two = block(b, real, n, 1, s1, dp1)
                for f, g2 in zip(one, two):
                    f()
                    g2()
        out_copy(a).start()

        @pl.when(real > 0)
        def _():
            out_copy(b).start()
        return carry

    lax.fori_loop(0, count, row_pair, 0)
    for i in range(nt // 4):
        for z in range(2):
            frm = slice((2 * i + z) * W, (2 * i + z + 1) * W)
            to = slice(i * W, (i + 1) * W)
            kvt_ref[0, z, :, to] = (acc[:HD, frm] * inv_root).astype(jnp.bfloat16)
            kvt_ref[1, z, :, to] = acc[HD:, frm].astype(jnp.bfloat16)

    def finish(i, carry):
        out_copy(i).wait()
        return carry
    lax.fori_loop(0, nt, finish, 0)


def attention(queries, out_grad, key_values, ratio, pair, item, image):
    L = queries.shape[1]
    nt = L // TILE
    hbm = pl.BlockSpec(memory_space=pl.ANY)
    wide = pltpu.VMEM((2 * TILE, L), jnp.float32)
    low = pltpu.VMEM((L, 2 * HD), jnp.bfloat16)
    return pl.pallas_call(
        attention_kernel,
        out_shape=[jax.ShapeDtypeStruct(queries.shape, jnp.bfloat16),
                   jax.ShapeDtypeStruct((2, 2, HD, L // 2), jnp.bfloat16)],
        in_specs=[hbm] * 7,
        out_specs=[hbm, pl.BlockSpec(memory_space=pltpu.VMEM)],
        scratch_shapes=[low, low, low, pltpu.VMEM((L + TILE, 2 * HD), jnp.bfloat16), wide, wide, wide, wide,
            pltpu.VMEM((2 * HD, L), jnp.float32),
            pltpu.SMEM(ratio.shape, jnp.float32),
            pltpu.SMEM(pair.shape, jnp.int32),
            pltpu.SMEM(item.shape, jnp.int32),
            pltpu.SMEM(image.shape, jnp.int32),
            pltpu.SMEM((nt,), jnp.int32),
            pltpu.SMEM((nt,), jnp.int32),
            pltpu.SMEM((nt,), jnp.int32),
            pltpu.SMEM((nt + 1,), jnp.int32),
            pltpu.SMEM((3 * (nt + 1),), jnp.int32),
            pltpu.SMEM((2 * ratio.shape[1],), jnp.float32),
            pltpu.SemaphoreType.DMA((4,)), pltpu.SemaphoreType.DMA((3,)), pltpu.SemaphoreType.DMA((nt,)),
        ],
        compiler_params=pltpu.CompilerParams(vmem_limit_bytes=56 << 20),
        cost_estimate=pl.CostEstimate(flops=10 * 10**9, bytes_accessed=8 << 20, transcendentals=0),
        name="attention",
    )(ratio, pair, item, image, queries, out_grad, key_values)


CHUNKS = 4
PARTS = CHUNKS // 2
TIMES = ((0, 1), (1, 1), (2.2, 1), (3.3, 1), (5.4, 1), (6.5, 1))
SHARE = (0.5, 0.5, 0.5, 0.5)
MESH = pl.DeviceIdType.MESH
F32 = jnp.float32
BF16 = jnp.bfloat16


def exchange_kernel(kvt, x_own, x1, x2, x3, out_ref,
                    own, core_in, part, z_in, heads, xs, prod, y_out, y_in, final, turned, landed,
                    core_s, core_r, z_s, z_r, right_s, right_r, left_s, left_r,
                    fr_s, fr_r, fl_s, fl_r, y_s, y_r,
                    load_sem, x_sem, xs_s, xs_r, turn_s, turn_r, out_s, out_r):
    dp = lax.axis_index("dp")
    tp = lax.axis_index("tp")
    y = dp // 4
    zh = dp % 4
    x = tp // 4
    zl = tp // 2 % 2
    c = tp % 2
    rows, length = z_in.shape[1:]
    cols = xs.shape[3]
    half = length // 2
    sibling = (dp, x * 4 + zl * 2 + (1 - c))
    across = (dp, x * 4 + (1 - zl) * 2 + c)
    around = [(lax.rem(y + j, 4) * 4 + zh, tp) for j in range(4)]
    beside = [(dp, lax.rem(x + j, 4) * 4 + zl * 2 + c) for j in range(4)]
    right, left = beside[1], beside[3]

    load = pltpu.make_async_copy(kvt.at[c], own, load_sem)
    load.start()
    x_loads = []
    for j, src in enumerate((x_own, x1, x2, x3)):
        cp = pltpu.make_async_copy(src, xs.at[lax.rem(x + 4 - j, 4), c], x_sem.at[j])
        cp.start()
        x_loads.append(cp)

    barrier = pltpu.get_barrier_semaphore()
    for partner in (sibling, across, *beside[1:], *around[1:]):
        pl.semaphore_signal(barrier, 1, device_id=partner, device_id_type=MESH)

    def dest(u, h):
        return y * 4 + h, x * 4 + c * 2 + u

    def is_other(d, t):
        return jnp.logical_or(d != dp, t != tp)

    def greet(d, t, n):
        other = is_other(d, t)

        @pl.when(other)
        def _():
            pl.semaphore_signal(barrier, 1, device_id=(d, t), device_id_type=MESH)
        return n + jnp.where(other, 1, 0)

    n = lax.fori_loop(0, 8, lambda i, n: greet(*dest(i % 2, i // 2), n), jnp.int32(8))
    n = lax.fori_loop(0, 8, lambda i, n: greet(y * 4 + i // 2, x * 4 + i % 2 * 2 + zl, n), n)
    pl.semaphore_wait(barrier, n)

    started = []

    def send(src, dst, ss, rs, to):
        cp = pltpu.make_async_remote_copy(src_ref=src, dst_ref=dst, send_sem=ss, recv_sem=rs,
                                          device_id=to, device_id_type=MESH)
        cp.start()
        started.append(cp)
        return cp

    def cut(k):
        return pl.ds(k * rows, rows)

    core = [send(kvt.at[1 - c, :, cut(k)], core_in.at[k], core_s.at[k], core_r.at[k], sibling)
            for k in range(CHUNKS)]
    load.wait()

    zc, rc, lc, frc, flc, yc, tc, xc = ([] for _ in range(8))

    def share(j):
        x_loads[j].wait()
        here = xs.at[lax.rem(x + 4 - j, 4), c]
        xc.append(send(here, here, xs_s.at[j], xs_r.at[j], sibling))

    def reduce_core(k):
        core[k].wait_recv()
        part[k] = (own[1 - zl, cut(k)].astype(F32) + core_in[k, 1 - zl].astype(F32)).astype(BF16)
        zc.append(send(part.at[k], z_in.at[k], z_s.at[k], z_r.at[k], across))

    def reduce_z(k):
        zc[k].wait_recv()
        heads[k, x] = (own[zl, cut(k)].astype(F32) + core_in[k, zl].astype(F32) + z_in[k].astype(F32)).astype(BF16)
        here = heads.at[k, x]
        rc.append(send(here, here, right_s.at[k], right_r.at[k], right))
        lc.append(send(here, here, left_s.at[k], left_r.at[k], left))

    def forward(k):
        rc[k].wait_recv()
        a = heads.at[k, lax.rem(x + 3, 4), :, pl.ds(0, half)]
        frc.append(send(a, a, fr_s.at[k], fr_r.at[k], right))
        lc[k].wait_recv()
        b = heads.at[k, lax.rem(x + 1, 4), :, pl.ds(half, half)]
        flc.append(send(b, b, fl_s.at[k], fl_r.at[k], left))

    def multiply(k):
        frc[k].wait_recv()
        flc[k].wait_recv()
        if k == 0:
            for cp in xc:
                cp.wait_recv()
        lhs = heads[k].reshape(4 * rows, length)
        res = jnp.dot(lhs, xs[...].reshape(length, cols), preferred_element_type=F32)
        wide = cols // 4
        for q in range(4):
            prod[k, q] = res[:, q * wide:(q + 1) * wide]
        sent = []
        for j in (2, 1, 3):
            y_out[k, j - 1] = prod[k, lax.rem(y + j, 4)].astype(BF16)
            sent.append(send(y_out.at[k, j - 1], y_in.at[k, j - 1], y_s.at[k, j - 1], y_r.at[k, j - 1], around[j]))
        yc.append(sent)

    spot = zh * 2 + zl

    def out_copy(k, q):
        d, t = dest(k // PARTS, lax.rem(x + 4 - q, 4))
        return d, t, pltpu.make_async_remote_copy(
            src_ref=turned.at[k, q], dst_ref=landed.at[spot, k % PARTS], send_sem=out_s.at[k * 4 + q],
            recv_sem=out_r.at[spot, k % PARTS], device_id=(d, t), device_id_type=MESH)

    def deliver(k):
        for cp in yc[k]:
            cp.wait_recv()
        total = (prod[k, y] + y_in[k, 0].astype(F32) + y_in[k, 1].astype(F32) + y_in[k, 2].astype(F32)).astype(BF16)
        for h in range(4):
            final[k, h] = total[h * rows:(h + 1) * rows]
        turned[k, 0] = final[k, x]
        tc.append([send(final.at[k, lax.rem(x + j, 4)], turned.at[k, j], turn_s.at[k, j - 1], turn_r.at[k, j - 1],
                        beside[j]) for j in (2, 1, 3)])

    def scatter(k):
        for cp in tc[k]:
            cp.wait_recv()

        def one(q, carry):
            d, t, cp = out_copy(k, q)
            other = is_other(d, t)

            @pl.when(other)
            def _():
                cp.start()

            @pl.when(jnp.logical_not(other))
            def _():
                pltpu.make_async_copy(turned.at[k, q], landed.at[spot, k % PARTS], out_r.at[spot, k % PARTS]).start()
            return carry
        lax.fori_loop(0, 4, one, 0)

    stages = (reduce_core, reduce_z, forward, multiply, deliver, scatter)
    order = sorted((start + k * gap, i, k) for i, (start, gap) in enumerate(TIMES) for k in range(CHUNKS))
    order = sorted(order + [(SHARE[j], -1, j) for j in range(4)])
    for _, i, k in order:
        share(k) if i < 0 else stages[i](k)

    def collect(i, total):
        new = []
        for p in range(PARTS):
            pltpu.make_async_copy(landed.at[i, p], landed.at[i, p], out_r.at[i, p]).wait()
            new.append(total[p] + landed[i, p].astype(F32))
        return tuple(new)

    zero = jnp.zeros((rows, cols // 4), F32)
    sums = lax.fori_loop(0, 8, collect, (zero,) * PARTS)
    for p in range(PARTS):
        out_ref[p * rows:(p + 1) * rows] = sums[p]

    for cp in started:
        cp.wait_send()

    def drain(j, carry):
        d, t, cp = out_copy(j // 4, j % 4)

        @pl.when(is_other(d, t))
        def _():
            cp.wait_send()
        return carry
    lax.fori_loop(0, 4 * CHUNKS, drain, 0)


def exchange(kvt, x_own, others):
    length = kvt.shape[3]
    cols = x_own.shape[1]
    rows = HD // CHUNKS
    sem = pltpu.SemaphoreType.DMA
    n = CHUNKS
    return pl.pallas_call(
        exchange_kernel,
        out_shape=jax.ShapeDtypeStruct((PARTS * rows, cols // 4), F32),
        in_specs=[pl.BlockSpec(memory_space=pl.ANY)] * 5,
        out_specs=pl.BlockSpec(memory_space=pltpu.VMEM),
        scratch_shapes=[
            pltpu.VMEM((2, HD, length), BF16), pltpu.VMEM((n, 2, rows, length), BF16),
            pltpu.VMEM((n, rows, length), BF16), pltpu.VMEM((n, rows, length), BF16),
            pltpu.VMEM((n, 4, rows, length), BF16), pltpu.VMEM((4, 2, TILE, cols), BF16),
            pltpu.VMEM((n, 4, 4 * rows, cols // 4), F32),
            pltpu.VMEM((n, 3, 4 * rows, cols // 4), BF16), pltpu.VMEM((n, 3, 4 * rows, cols // 4), BF16),
            pltpu.VMEM((n, 4, rows, cols // 4), BF16), pltpu.VMEM((n, 4, rows, cols // 4), BF16),
            pltpu.VMEM((8, PARTS, rows, cols // 4), BF16),
        ] + [sem((n,))] * 12 + [sem((n, 3))] * 2 + [sem, sem((4,)), sem((4,)), sem((4,)),
                                                    sem((n, 3)), sem((n, 3)), sem((4 * n,)), sem((8, PARTS))],
        compiler_params=pltpu.CompilerParams(collective_id=0, has_side_effects=True, vmem_limit_bytes=40 << 20),
        cost_estimate=pl.CostEstimate(flops=10**9, bytes_accessed=8 << 20, transcendentals=0),
        name="exchange",
    )(kvt, x_own, *others)


def deal_kernel(x_in, *outs):
    x = lax.axis_index("tp") // 4
    wide = outs[0].shape[1] // 4
    for j in range(4):
        for i in range(4):
            cols = pl.ds(pl.multiple_of((4 * i + lax.rem(x + j, 4)) * wide, wide), wide)
            outs[j][:, i * wide:(i + 1) * wide] = x_in[:, cols]


def deal(rows):
    vmem = pl.BlockSpec(memory_space=pltpu.VMEM)
    shape = jax.ShapeDtypeStruct((rows.shape[0], rows.shape[1] // 4), BF16)
    return pl.pallas_call(deal_kernel, out_shape=[shape] * 4, in_specs=[vmem], out_specs=[vmem] * 4, name="deal")(rows)


def local(input_rows, queries, key_values, out_grad, item_logratio, pair_ids, tile_item, tile_image):
    rows = input_rows[0]
    others = []
    mine, *blocks = deal(rows)
    for dx, block in zip(range(1, 4), blocks):
        others.append(lax.ppermute(block, "tp", [(a, (a + 4 * dx) % 16) for a in range(16)]))
    dq, kvt = attention(queries, out_grad, key_values, item_logratio, pair_ids, tile_item, tile_image)
    return dq, exchange(kvt, mine, others).T


def solution(mesh):
    in_specs = (P("dp", "tp", None), P("dp", None, "tp"), P("dp", None, None), P("dp", None, "tp"),
                P("dp", None), P("dp", None), P("dp", None), P("dp", None))
    out_specs = (P("dp", None, "tp"), P("dp", "tp"))
    return jax.shard_map(local, mesh=mesh, in_specs=in_specs, out_specs=out_specs, check_vma=False)
```

```python
import functools, math
import jax, jax.numpy as jnp
from jax import lax
from jax.experimental import pallas as pl
from jax.experimental.pallas import tpu as pltpu

from jax.sharding import PartitionSpec as P

KVH = 4; HD = 128; TILE = 128; BETA = 0.1
MASKED = -1e30
LOG2E = 1.4426950408889634

def attention_kernel(ratio_h, pair_h, item_h, image_h, q_hbm, og_hbm, kv_hbm, dq_hbm, kvt_ref,
                     kv, q_ref, og_ref, dq_ref, s0, s1, dp0, dp1, acc, ratio, pair, item, image,
                     lo_s, hi_s, n_s, spot, order, work, z_s, small_sem, big_sem, dq_sem):
    group = lax.axis_size("tp") // KVH
    g = lax.axis_index("tp") // group
    nt = item.shape[1]
    items = ratio.shape[1]
    small = [pltpu.make_async_copy(a, b, small_sem.at[i])
             for i, (a, b) in enumerate(((ratio_h, ratio), (pair_h, pair), (item_h, item), (image_h, image)))]
    for cp in small:
        cp.start()
    big = [pltpu.make_async_copy(kv_hbm.at[0, :, pl.ds(pl.multiple_of(g * 2 * HD, 2 * HD), 2 * HD)], kv, big_sem.at[0]),
           pltpu.make_async_copy(q_hbm.at[0], q_ref, big_sem.at[1]),
           pltpu.make_async_copy(og_hbm.at[0], og_ref, big_sem.at[2])]
    for cp in big:
        cp.start()
    inv_root = 1.0 / math.sqrt(HD)
    c2 = inv_root * LOG2E
    W = 2 * TILE
    acc[...] = jnp.zeros_like(acc)
    for cp in small:
        cp.wait()
    lo_s[0] = 0
    for i in range(1, nt):
        lo_s[i] = jnp.where(item[0, i] == item[0, i - 1], lo_s[i - 1], i)
    hi_s[nt - 1] = nt - 1
    for i in reversed(range(nt - 1)):
        same = (image[0, i] > 0) & (image[0, i] == image[0, i + 1]) & (item[0, i] == item[0, i + 1])
        hi_s[i] = jnp.where(same, hi_s[i + 1], i)
    for a in range(items):
        other = jnp.float32(0.0)
        p = jnp.float32(1.0)
        for b in range(items):
            if b != a:
                same = pair[0, a] == pair[0, b]
                other = other + jnp.where(same, ratio[0, b], 0.0)
                if a < b:
                    p = jnp.where(same, -1.0, p)
        z_s[a] = BETA * p * (other - ratio[0, a])
        z_s[items + a] = p

    for i in range(nt):
        n_s[i] = (hi_s[i] - lo_s[i] + 2) // 2

    for n in range(nt // 2 + 1):
        spot[n] = 0
    for i in range(nt):
        spot[n_s[i]] = spot[n_s[i]] + 1
    start = jnp.int32(0)
    for n in reversed(range(1, nt // 2 + 1)):
        here = spot[n]
        spot[n] = start
        start = start + here
    for i in range(nt):
        order[spot[n_s[i]]] = i
        spot[n_s[i]] = spot[n_s[i]] + 1

    def match(t, carry):
        i, w = carry
        a = order[jnp.minimum(i, nt - 1)]
        b = order[jnp.minimum(i + 1, nt - 1)]
        both = (i + 1 < nt) & (n_s[a] - n_s[b] <= 1)
        more = i < nt
        work[3 * w] = a
        work[3 * w + 1] = jnp.where(both, b, a)
        work[3 * w + 2] = jnp.where(both, 1, 0)
        return i + jnp.where(both, 2, 1), w + jnp.where(more, 1, 0)

    _, count = lax.fori_loop(0, nt, match, (jnp.int32(0), jnp.int32(0)))
    for cp in big:
        cp.wait()

    def block(I, real, n, spare, s_scr, dp_scr):
        lo = lo_s[I]
        hi = hi_s[I]
        img = image[0, I]
        it = item[0, I]
        r0 = pl.multiple_of(I * TILE, TILE)
        st = pl.multiple_of(jnp.clip(hi + 1 - 2 * n, 0, nt - 2 * n) * TILE, TILE)
        first = lo * TILE - st
        v = {}

        def stage1():
            qi = q_ref[pl.ds(r0, TILE), :]
            q2 = jnp.concatenate([qi[:, :HD], qi[:, HD:]], axis=0)
            coef = z_s[items + it] * real.astype(jnp.float32) / (1.0 + jnp.exp(jnp.full((8, HD), z_s[it], jnp.float32)))
            coef = jnp.concatenate([coef[:1], coef[:1]], axis=1)
            wi = (og_ref[pl.ds(r0, TILE), :].astype(jnp.float32) * coef).astype(jnp.bfloat16)
            w2 = jnp.concatenate([wi[:, :HD], wi[:, HD:]], axis=0)
            v["q2t"] = q2.T
            v["w2t"] = w2.T
            row = lax.broadcasted_iota(jnp.int32, (TILE, 1), 0)
            row = jnp.concatenate([row, row], axis=0)
            last = jnp.where(img > 0, jnp.full((2 * TILE, 1), (hi + 1) * TILE - 1 - st), r0 - st + row)
            m = None
            for ch in range(n):
                rows = pl.ds(st + ch * W, W)
                s = lax.dot_general(q2, kv[rows, :HD], (((1,), (1,)), ((), ())), preferred_element_type=jnp.float32)
                if ch <= spare or ch >= n - 2:
                    col = lax.broadcasted_iota(jnp.int32, (1, W), 1) + ch * W
                    s = jnp.where(jnp.where(col >= first, col, nt * TILE) <= last, s, MASKED)
                s_scr[:, ch * W:(ch + 1) * W] = s
                mm = jnp.maximum(s[:, :HD], s[:, HD:])
                m = mm if m is None else jnp.maximum(m, mm)
                dp_scr[:, ch * W:(ch + 1) * W] = lax.dot_general(
                    w2, kv[rows, HD:], (((1,), (1,)), ((), ())), preferred_element_type=jnp.float32)
            v["m"] = jnp.max(m, axis=1, keepdims=True) * c2

        def stage2():
            mr = v["m"]
            l = r = None
            for ch in range(n):
                cols = slice(ch * W, (ch + 1) * W)
                p = jnp.exp2(s_scr[:, cols] * c2 - mr)
                s_scr[:, cols] = p
                pd = p * dp_scr[:, cols]
                ll = p[:, :HD] + p[:, HD:]
                rr = pd[:, :HD] + pd[:, HD:]
                l = ll if l is None else l + ll
                r = rr if r is None else r + rr
            v["inv"] = 1.0 / jnp.sum(l, axis=1, keepdims=True)
            v["rd"] = jnp.sum(r, axis=1, keepdims=True) * v["inv"]

        def stage3():
            inv, rd = v["inv"], v["rd"]
            dq = None
            for ch in range(n):
                rows = pl.ds(st + ch * W, W)
                cols = slice(ch * W, (ch + 1) * W)
                at = s_scr[:, cols] * inv
                ds = (at * (dp_scr[:, cols] - rd)).astype(jnp.bfloat16)
                at = at.astype(jnp.bfloat16)
                d = jnp.dot(ds, kv[rows, :HD], preferred_element_type=jnp.float32)
                dq = d if dq is None else dq + d
                acc[:HD, rows] += jnp.dot(v["q2t"], ds, preferred_element_type=jnp.float32)
                acc[HD:, rows] += jnp.dot(v["w2t"], at, preferred_element_type=jnp.float32)
            dq = (dq * inv_root).astype(jnp.bfloat16)
            to = pl.ds(pl.multiple_of(jnp.where(real > 0, I, nt) * TILE, TILE), TILE)
            dq_ref[to, :HD] = dq[:TILE]
            dq_ref[to, HD:] = dq[TILE:]

        return stage1, stage2, stage3

    def out_copy(i):
        here = pl.ds(pl.multiple_of(i * TILE, TILE), TILE)
        return pltpu.make_async_copy(dq_ref.at[here], dq_hbm.at[0, here], dq_sem.at[i])

    def row_pair(j, carry):
        a, b, real = work[3 * j], work[3 * j + 1], work[3 * j + 2]
        n_here = n_s[a]
        for n in range(1, nt // 2 + 1):
            @pl.when(n_here == n)
            def _():
                one = block(a, jnp.int32(1), n, 1, s0, dp0)
                two = block(b, real, n, 1, s1, dp1)
                for f, g2 in zip(one, two):
                    f()
                    g2()
        out_copy(a).start()

        @pl.when(real > 0)
        def _():
            out_copy(b).start()
        return carry

    lax.fori_loop(0, count, row_pair, 0)
    for i in range(nt // 4):
        for z in range(2):
            frm = slice((2 * i + z) * W, (2 * i + z + 1) * W)
            to = slice(i * W, (i + 1) * W)
            kvt_ref[0, z, :, to] = (acc[:HD, frm] * inv_root).astype(jnp.bfloat16)
            kvt_ref[1, z, :, to] = acc[HD:, frm].astype(jnp.bfloat16)

    def finish(i, carry):
        out_copy(i).wait()
        return carry
    lax.fori_loop(0, nt, finish, 0)


def attention(queries, out_grad, key_values, ratio, pair, item, image):
    L = queries.shape[1]
    nt = L // TILE
    hbm = pl.BlockSpec(memory_space=pl.ANY)
    wide = pltpu.VMEM((2 * TILE, L), jnp.float32)
    low = pltpu.VMEM((L, 2 * HD), jnp.bfloat16)
    return pl.pallas_call(
        attention_kernel,
        out_shape=[jax.ShapeDtypeStruct(queries.shape, jnp.bfloat16),
                   jax.ShapeDtypeStruct((2, 2, HD, L // 2), jnp.bfloat16)],
        in_specs=[hbm] * 7,
        out_specs=[hbm, pl.BlockSpec(memory_space=pltpu.VMEM)],
        scratch_shapes=[low, low, low, pltpu.VMEM((L + TILE, 2 * HD), jnp.bfloat16), wide, wide, wide, wide,
            pltpu.VMEM((2 * HD, L), jnp.float32),
            pltpu.SMEM(ratio.shape, jnp.float32),
            pltpu.SMEM(pair.shape, jnp.int32),
            pltpu.SMEM(item.shape, jnp.int32),
            pltpu.SMEM(image.shape, jnp.int32),
            pltpu.SMEM((nt,), jnp.int32),
            pltpu.SMEM((nt,), jnp.int32),
            pltpu.SMEM((nt,), jnp.int32),
            pltpu.SMEM((nt // 2 + 1,), jnp.int32),
            pltpu.SMEM((nt + 1,), jnp.int32),
            pltpu.SMEM((3 * (nt + 1),), jnp.int32),
            pltpu.SMEM((2 * ratio.shape[1],), jnp.float32),
            pltpu.SemaphoreType.DMA((4,)), pltpu.SemaphoreType.DMA((3,)), pltpu.SemaphoreType.DMA((nt,)),
        ],
        compiler_params=pltpu.CompilerParams(vmem_limit_bytes=56 << 20),
        cost_estimate=pl.CostEstimate(flops=10 * 10**9, bytes_accessed=8 << 20, transcendentals=0),
        name="attention",
    )(ratio, pair, item, image, queries, out_grad, key_values)


CHUNKS = 4
PARTS = CHUNKS // 2
TIMES = ((0, 1), (1, 1), (3.2, 1), (5.4, 1), (7.5, 1))
SHARE = (0.5, 0.5, 0.5, 0.5)
MESH = pl.DeviceIdType.MESH
F32 = jnp.float32
BF16 = jnp.bfloat16


def exchange_kernel(kvt, x_own, x1, x2, x3, out_ref,
                    own, core_in, part, z_in, heads, xs, prod, y_out, y_in, final, turned, landed,
                    core_s, core_r, z_s, z_r, x_s, x_r, y_s, y_r,
                    load_sem, x_sem, xs_s, xs_r, turn_s, turn_r, out_s, out_r):
    dp = lax.axis_index("dp")
    tp = lax.axis_index("tp")
    y = dp // 4
    zh = dp % 4
    x = tp // 4
    zl = tp // 2 % 2
    c = tp % 2
    rows, length = z_in.shape[1:]
    cols = xs.shape[3]
    sibling = (dp, x * 4 + zl * 2 + (1 - c))
    across = (dp, x * 4 + (1 - zl) * 2 + c)
    around = [(lax.rem(y + j, 4) * 4 + zh, tp) for j in range(4)]
    beside = [(dp, lax.rem(x + j, 4) * 4 + zl * 2 + c) for j in range(4)]

    load = pltpu.make_async_copy(kvt.at[c], own, load_sem)
    load.start()
    x_loads = []
    for j, src in enumerate((x_own, x1, x2, x3)):
        cp = pltpu.make_async_copy(src, xs.at[lax.rem(x + 4 - j, 4), c], x_sem.at[j])
        cp.start()
        x_loads.append(cp)

    barrier = pltpu.get_barrier_semaphore()
    for partner in (sibling, across, *beside[1:], *around[1:]):
        pl.semaphore_signal(barrier, 1, device_id=partner, device_id_type=MESH)

    def dest(u, h):
        return y * 4 + h, x * 4 + c * 2 + u

    def is_other(d, t):
        return jnp.logical_or(d != dp, t != tp)

    def greet(d, t, n):
        other = is_other(d, t)

        @pl.when(other)
        def _():
            pl.semaphore_signal(barrier, 1, device_id=(d, t), device_id_type=MESH)
        return n + jnp.where(other, 1, 0)

    n = lax.fori_loop(0, 8, lambda i, n: greet(*dest(i % 2, i // 2), n), jnp.int32(8))
    n = lax.fori_loop(0, 8, lambda i, n: greet(y * 4 + i // 2, x * 4 + i % 2 * 2 + zl, n), n)
    pl.semaphore_wait(barrier, n)

    started = []

    def send(src, dst, ss, rs, to):
        cp = pltpu.make_async_remote_copy(src_ref=src, dst_ref=dst, send_sem=ss, recv_sem=rs,
                                          device_id=to, device_id_type=MESH)
        cp.start()
        started.append(cp)
        return cp

    def cut(k):
        return pl.ds(k * rows, rows)

    core = [send(kvt.at[1 - c, :, cut(k)], core_in.at[k], core_s.at[k], core_r.at[k], sibling)
            for k in range(CHUNKS)]
    load.wait()

    zc, hc, yc, tc, xc = ([] for _ in range(5))

    def share(j):
        x_loads[j].wait()
        here = xs.at[lax.rem(x + 4 - j, 4), c]
        xc.append(send(here, here, xs_s.at[j], xs_r.at[j], sibling))

    def reduce_core(k):
        core[k].wait_recv()
        part[k] = (own[1 - zl, cut(k)].astype(F32) + core_in[k, 1 - zl].astype(F32)).astype(BF16)
        zc.append(send(part.at[k], z_in.at[k], z_s.at[k], z_r.at[k], across))

    def reduce_z(k):
        zc[k].wait_recv()
        heads[k, x] = (own[zl, cut(k)].astype(F32) + core_in[k, zl].astype(F32) + z_in[k].astype(F32)).astype(BF16)
        here = heads.at[k, x]
        hc.append([send(here, here, x_s.at[k, j - 1], x_r.at[k, j - 1], beside[j]) for j in (2, 1, 3)])

    def multiply(k):
        for cp in hc[k]:
            cp.wait_recv()
        if k == 0:
            for cp in xc:
                cp.wait_recv()
        lhs = heads[k].reshape(4 * rows, length)
        res = jnp.dot(lhs, xs[...].reshape(length, cols), preferred_element_type=F32)
        wide = cols // 4
        for q in range(4):
            prod[k, q] = res[:, q * wide:(q + 1) * wide]
        sent = []
        for j in (2, 1, 3):
            y_out[k, j - 1] = prod[k, lax.rem(y + j, 4)].astype(BF16)
            sent.append(send(y_out.at[k, j - 1], y_in.at[k, j - 1], y_s.at[k, j - 1], y_r.at[k, j - 1], around[j]))
        yc.append(sent)

    spot = zh * 2 + zl

    def out_copy(k, q):
        d, t = dest(k // PARTS, lax.rem(x + 4 - q, 4))
        return d, t, pltpu.make_async_remote_copy(
            src_ref=turned.at[k, q], dst_ref=landed.at[spot, k % PARTS], send_sem=out_s.at[k * 4 + q],
            recv_sem=out_r.at[spot, k % PARTS], device_id=(d, t), device_id_type=MESH)

    def deliver(k):
        for cp in yc[k]:
            cp.wait_recv()
        total = (prod[k, y] + y_in[k, 0].astype(F32) + y_in[k, 1].astype(F32) + y_in[k, 2].astype(F32)).astype(BF16)
        for h in range(4):
            final[k, h] = total[h * rows:(h + 1) * rows]
        turned[k, 0] = final[k, x]
        tc.append([send(final.at[k, lax.rem(x + j, 4)], turned.at[k, j], turn_s.at[k, j - 1], turn_r.at[k, j - 1],
                        beside[j]) for j in (2, 1, 3)])

    def scatter(k):
        for cp in tc[k]:
            cp.wait_recv()

        def one(q, carry):
            d, t, cp = out_copy(k, q)
            other = is_other(d, t)

            @pl.when(other)
            def _():
                cp.start()

            @pl.when(jnp.logical_not(other))
            def _():
                pltpu.make_async_copy(turned.at[k, q], landed.at[spot, k % PARTS], out_r.at[spot, k % PARTS]).start()
            return carry
        lax.fori_loop(0, 4, one, 0)

    stages = (reduce_core, reduce_z, multiply, deliver, scatter)
    order = sorted((start + k * gap, i, k) for i, (start, gap) in enumerate(TIMES) for k in range(CHUNKS))
    order = sorted(order + [(SHARE[j], -1, j) for j in range(4)])
    for _, i, k in order:
        share(k) if i < 0 else stages[i](k)

    def collect(i, total):
        new = []
        for p in range(PARTS):
            pltpu.make_async_copy(landed.at[i, p], landed.at[i, p], out_r.at[i, p]).wait()
            new.append(total[p] + landed[i, p].astype(F32))
        return tuple(new)

    zero = jnp.zeros((rows, cols // 4), F32)
    sums = lax.fori_loop(0, 8, collect, (zero,) * PARTS)
    for p in range(PARTS):
        out_ref[p * rows:(p + 1) * rows] = sums[p]

    for cp in started:
        cp.wait_send()

    def drain(j, carry):
        d, t, cp = out_copy(j // 4, j % 4)

        @pl.when(is_other(d, t))
        def _():
            cp.wait_send()
        return carry
    lax.fori_loop(0, 4 * CHUNKS, drain, 0)


def exchange(kvt, x_own, others):
    length = kvt.shape[3]
    cols = x_own.shape[1]
    rows = HD // CHUNKS
    sem = pltpu.SemaphoreType.DMA
    n = CHUNKS
    return pl.pallas_call(
        exchange_kernel,
        out_shape=jax.ShapeDtypeStruct((PARTS * rows, cols // 4), F32),
        in_specs=[pl.BlockSpec(memory_space=pl.ANY)] * 5,
        out_specs=pl.BlockSpec(memory_space=pltpu.VMEM),
        scratch_shapes=[
            pltpu.VMEM((2, HD, length), BF16), pltpu.VMEM((n, 2, rows, length), BF16),
            pltpu.VMEM((n, rows, length), BF16), pltpu.VMEM((n, rows, length), BF16),
            pltpu.VMEM((n, 4, rows, length), BF16), pltpu.VMEM((4, 2, TILE, cols), BF16),
            pltpu.VMEM((n, 4, 4 * rows, cols // 4), F32),
            pltpu.VMEM((n, 3, 4 * rows, cols // 4), BF16), pltpu.VMEM((n, 3, 4 * rows, cols // 4), BF16),
            pltpu.VMEM((n, 4, rows, cols // 4), BF16), pltpu.VMEM((n, 4, rows, cols // 4), BF16),
            pltpu.VMEM((8, PARTS, rows, cols // 4), BF16),
        ] + [sem((n,))] * 4 + [sem((n, 3))] * 4 + [sem, sem((4,)), sem((4,)), sem((4,)),
                                                    sem((n, 3)), sem((n, 3)), sem((4 * n,)), sem((8, PARTS))],
        compiler_params=pltpu.CompilerParams(collective_id=0, has_side_effects=True, vmem_limit_bytes=40 << 20),
        cost_estimate=pl.CostEstimate(flops=10**9, bytes_accessed=8 << 20, transcendentals=0),
        name="exchange",
    )(kvt, x_own, *others)


def deal_kernel(x_in, *outs):
    x = lax.axis_index("tp") // 4
    wide = outs[0].shape[1] // 4
    for j in range(4):
        for i in range(4):
            cols = pl.ds(pl.multiple_of((4 * i + lax.rem(x + j, 4)) * wide, wide), wide)
            outs[j][:, i * wide:(i + 1) * wide] = x_in[:, cols]


def deal(rows):
    vmem = pl.BlockSpec(memory_space=pltpu.VMEM)
    shape = jax.ShapeDtypeStruct((rows.shape[0], rows.shape[1] // 4), BF16)
    return pl.pallas_call(deal_kernel, out_shape=[shape] * 4, in_specs=[vmem], out_specs=[vmem] * 4, name="deal")(rows)


def local(input_rows, queries, key_values, out_grad, item_logratio, pair_ids, tile_item, tile_image):
    rows = input_rows[0]
    others = []
    mine, *blocks = deal(rows)
    for dx, block in zip(range(1, 4), blocks):
        others.append(lax.ppermute(block, "tp", [(a, (a + 4 * dx) % 16) for a in range(16)]))
    dq, kvt = attention(queries, out_grad, key_values, item_logratio, pair_ids, tile_item, tile_image)
    return dq, exchange(kvt, mine, others).T


def solution(mesh):
    in_specs = (P("dp", "tp", None), P("dp", None, "tp"), P("dp", None, None), P("dp", None, "tp"),
                P("dp", None), P("dp", None), P("dp", None), P("dp", None))
    out_specs = (P("dp", None, "tp"), P("dp", "tp"))
    return jax.shard_map(local, mesh=mesh, in_specs=in_specs, out_specs=out_specs, check_vma=False)
```

```python
import functools, math
import jax, jax.numpy as jnp
from jax import lax
from jax.experimental import pallas as pl
from jax.experimental.pallas import tpu as pltpu

from jax.sharding import PartitionSpec as P

KVH = 4; HD = 128; TILE = 128; BETA = 0.1
MASKED = -1e30
LOG2E = 1.4426950408889634

def attention_kernel(ratio_h, pair_h, item_h, image_h, q_hbm, og_hbm, kv_hbm, dq_hbm, kvt_hbm,
                     kvt_ref, kv, q_ref, og_ref, dq_ref, s0, s1, dp0, dp1, acc, ratio, pair, item, image,
                     lo_s, hi_s, n_s, spot, order, work, z_s, small_sem, big_sem, dq_sem, kvt_sem):
    group = lax.axis_size("tp") // KVH
    g = lax.axis_index("tp") // group
    nt = item.shape[1]
    items = ratio.shape[1]
    small = [pltpu.make_async_copy(a, b, small_sem.at[i])
             for i, (a, b) in enumerate(((ratio_h, ratio), (pair_h, pair), (item_h, item), (image_h, image)))]
    for cp in small:
        cp.start()
    big = [pltpu.make_async_copy(kv_hbm.at[0, :, pl.ds(pl.multiple_of(g * 2 * HD, 2 * HD), 2 * HD)], kv, big_sem.at[0]),
           pltpu.make_async_copy(q_hbm.at[0], q_ref, big_sem.at[1]),
           pltpu.make_async_copy(og_hbm.at[0], og_ref, big_sem.at[2])]
    for cp in big:
        cp.start()
    inv_root = 1.0 / math.sqrt(HD)
    c2 = inv_root * LOG2E
    W = 2 * TILE
    acc[...] = jnp.zeros_like(acc)
    for cp in small:
        cp.wait()
    lo_s[0] = 0
    for i in range(1, nt):
        lo_s[i] = jnp.where(item[0, i] == item[0, i - 1], lo_s[i - 1], i)
    hi_s[nt - 1] = nt - 1
    for i in reversed(range(nt - 1)):
        same = (image[0, i] > 0) & (image[0, i] == image[0, i + 1]) & (item[0, i] == item[0, i + 1])
        hi_s[i] = jnp.where(same, hi_s[i + 1], i)
    for a in range(items):
        other = jnp.float32(0.0)
        p = jnp.float32(1.0)
        for b in range(items):
            if b != a:
                same = pair[0, a] == pair[0, b]
                other = other + jnp.where(same, ratio[0, b], 0.0)
                if a < b:
                    p = jnp.where(same, -1.0, p)
        z_s[a] = BETA * p * (other - ratio[0, a])
        z_s[items + a] = p

    for i in range(nt):
        n_s[i] = (hi_s[i] - lo_s[i] + 2) // 2

    for n in range(nt // 2 + 1):
        spot[n] = 0
    for i in range(nt):
        spot[n_s[i]] = spot[n_s[i]] + 1
    start = jnp.int32(0)
    for n in reversed(range(1, nt // 2 + 1)):
        here = spot[n]
        spot[n] = start
        start = start + here
    for i in range(nt):
        order[spot[n_s[i]]] = i
        spot[n_s[i]] = spot[n_s[i]] + 1

    def match(t, carry):
        i, w = carry
        a = order[jnp.minimum(i, nt - 1)]
        b = order[jnp.minimum(i + 1, nt - 1)]
        both = (i + 1 < nt) & (n_s[a] - n_s[b] <= 1)
        more = i < nt
        work[3 * w] = a
        work[3 * w + 1] = jnp.where(both, b, a)
        work[3 * w + 2] = jnp.where(both, 1, 0)
        return i + jnp.where(both, 2, 1), w + jnp.where(more, 1, 0)

    _, count = lax.fori_loop(0, nt, match, (jnp.int32(0), jnp.int32(0)))
    for cp in big:
        cp.wait()

    def block(I, real, n, spare, s_scr, dp_scr):
        lo = lo_s[I]
        hi = hi_s[I]
        img = image[0, I]
        it = item[0, I]
        r0 = pl.multiple_of(I * TILE, TILE)
        st = pl.multiple_of(jnp.clip(hi + 1 - 2 * n, 0, nt - 2 * n) * TILE, TILE)
        first = lo * TILE - st
        v = {}

        def stage1():
            qi = q_ref[pl.ds(r0, TILE), :]
            q2 = jnp.concatenate([qi[:, :HD], qi[:, HD:]], axis=0)
            coef = z_s[items + it] * real.astype(jnp.float32) / (1.0 + jnp.exp(jnp.full((8, HD), z_s[it], jnp.float32)))
            coef = jnp.concatenate([coef[:1], coef[:1]], axis=1)
            wi = (og_ref[pl.ds(r0, TILE), :].astype(jnp.float32) * coef).astype(jnp.bfloat16)
            w2 = jnp.concatenate([wi[:, :HD], wi[:, HD:]], axis=0)
            v["q2t"] = q2.T
            v["w2t"] = w2.T
            row = lax.broadcasted_iota(jnp.int32, (TILE, 1), 0)
            row = jnp.concatenate([row, row], axis=0)
            last = jnp.where(img > 0, jnp.full((2 * TILE, 1), (hi + 1) * TILE - 1 - st), r0 - st + row)
            m = None
            for ch in range(n):
                rows = pl.ds(st + ch * W, W)
                s = lax.dot_general(q2, kv[rows, :HD], (((1,), (1,)), ((), ())), preferred_element_type=jnp.float32)
                if ch <= spare or ch >= n - 2:
                    col = lax.broadcasted_iota(jnp.int32, (1, W), 1) + ch * W
                    s = jnp.where(jnp.where(col >= first, col, nt * TILE) <= last, s, MASKED)
                s_scr[:, ch * W:(ch + 1) * W] = s
                mm = jnp.maximum(s[:, :HD], s[:, HD:])
                m = mm if m is None else jnp.maximum(m, mm)
                dp_scr[:, ch * W:(ch + 1) * W] = lax.dot_general(
                    w2, kv[rows, HD:], (((1,), (1,)), ((), ())), preferred_element_type=jnp.float32)
            v["m"] = jnp.max(m, axis=1, keepdims=True) * c2

        def stage2():
            mr = v["m"]
            l = r = None
            for ch in range(n):
                cols = slice(ch * W, (ch + 1) * W)
                p = jnp.exp2(s_scr[:, cols] * c2 - mr)
                s_scr[:, cols] = p
                pd = p * dp_scr[:, cols]
                ll = p[:, :HD] + p[:, HD:]
                rr = pd[:, :HD] + pd[:, HD:]
                l = ll if l is None else l + ll
                r = rr if r is None else r + rr
            v["inv"] = 1.0 / jnp.sum(l, axis=1, keepdims=True)
            v["rd"] = jnp.sum(r, axis=1, keepdims=True) * v["inv"]

        def stage3():
            inv, rd = v["inv"], v["rd"]
            dq = None
            for ch in range(n):
                rows = pl.ds(st + ch * W, W)
                cols = slice(ch * W, (ch + 1) * W)
                at = s_scr[:, cols] * inv
                ds = (at * (dp_scr[:, cols] - rd)).astype(jnp.bfloat16)
                at = at.astype(jnp.bfloat16)
                d = jnp.dot(ds, kv[rows, :HD], preferred_element_type=jnp.float32)
                dq = d if dq is None else dq + d
                acc[:HD, rows] += jnp.dot(v["q2t"], ds, preferred_element_type=jnp.float32)
                acc[HD:, rows] += jnp.dot(v["w2t"], at, preferred_element_type=jnp.float32)
            dq = (dq * inv_root).astype(jnp.bfloat16)
            to = pl.ds(pl.multiple_of(jnp.where(real > 0, I, nt) * TILE, TILE), TILE)
            dq_ref[to, :HD] = dq[:TILE]
            dq_ref[to, HD:] = dq[TILE:]

        return stage1, stage2, stage3

    def out_copy(i):
        here = pl.ds(pl.multiple_of(i * TILE, TILE), TILE)
        return pltpu.make_async_copy(dq_ref.at[here], dq_hbm.at[0, here], dq_sem.at[i])

    def row_pair(j, carry):
        a, b, real = work[3 * j], work[3 * j + 1], work[3 * j + 2]
        n_here = n_s[a]
        for n in range(1, nt // 2 + 1):
            @pl.when(n_here == n)
            def _():
                one = block(a, jnp.int32(1), n, 1, s0, dp0)
                two = block(b, real, n, 1, s1, dp1)
                for f, g2 in zip(one, two):
                    f()
                    g2()
        out_copy(a).start()

        @pl.when(real > 0)
        def _():
            out_copy(b).start()
        return carry

    lax.fori_loop(0, count, row_pair, 0)
    kvt_out = []
    for part in range(2):
        for z in range(2):
            for i in range(nt // 4):
                frm = slice((2 * i + z) * W, (2 * i + z + 1) * W)
                block = acc[part * HD:(part + 1) * HD, frm]
                kvt_ref[part, z, :, i * W:(i + 1) * W] = (block if part else block * inv_root).astype(jnp.bfloat16)
            cp = pltpu.make_async_copy(kvt_ref.at[part, z], kvt_hbm.at[part, z], kvt_sem.at[part, z])
            cp.start()
            kvt_out.append(cp)

    def finish(i, carry):
        out_copy(i).wait()
        return carry
    lax.fori_loop(0, nt, finish, 0)
    for cp in kvt_out:
        cp.wait()


def attention(queries, out_grad, key_values, ratio, pair, item, image):
    L = queries.shape[1]
    nt = L // TILE
    hbm = pl.BlockSpec(memory_space=pl.ANY)
    wide = pltpu.VMEM((2 * TILE, L), jnp.float32)
    low = pltpu.VMEM((L, 2 * HD), jnp.bfloat16)
    return pl.pallas_call(
        attention_kernel,
        out_shape=[jax.ShapeDtypeStruct(queries.shape, jnp.bfloat16),
                   jax.ShapeDtypeStruct((2, 2, HD, L // 2), jnp.bfloat16)],
        in_specs=[hbm] * 7,
        out_specs=[hbm, hbm],
        scratch_shapes=[pltpu.VMEM((2, 2, HD, L // 2), jnp.bfloat16), low, low, low, pltpu.VMEM((L + TILE, 2 * HD), jnp.bfloat16), wide, wide, wide, wide,
            pltpu.VMEM((2 * HD, L), jnp.float32),
            pltpu.SMEM(ratio.shape, jnp.float32),
            pltpu.SMEM(pair.shape, jnp.int32),
            pltpu.SMEM(item.shape, jnp.int32),
            pltpu.SMEM(image.shape, jnp.int32),
            pltpu.SMEM((nt,), jnp.int32),
            pltpu.SMEM((nt,), jnp.int32),
            pltpu.SMEM((nt,), jnp.int32),
            pltpu.SMEM((nt // 2 + 1,), jnp.int32),
            pltpu.SMEM((nt + 1,), jnp.int32),
            pltpu.SMEM((3 * (nt + 1),), jnp.int32),
            pltpu.SMEM((2 * ratio.shape[1],), jnp.float32),
            pltpu.SemaphoreType.DMA((4,)), pltpu.SemaphoreType.DMA((3,)), pltpu.SemaphoreType.DMA((nt,)), pltpu.SemaphoreType.DMA((2, 2)),
        ],
        compiler_params=pltpu.CompilerParams(vmem_limit_bytes=56 << 20),
        cost_estimate=pl.CostEstimate(flops=10 * 10**9, bytes_accessed=8 << 20, transcendentals=0),
        name="attention",
    )(ratio, pair, item, image, queries, out_grad, key_values)


CHUNKS = 4
PARTS = CHUNKS // 2
TIMES = ((0, 1), (1, 1), (3.2, 1), (5.4, 1), (7.5, 1))
SHARE = (0.5, 0.5, 0.5, 0.5)
MESH = pl.DeviceIdType.MESH
F32 = jnp.float32
BF16 = jnp.bfloat16


def exchange_kernel(kvt, x_own, x1, x2, x3, out_ref,
                    own, core_in, part, z_in, heads, xs, prod, y_out, y_in, final, turned, landed,
                    core_s, core_r, z_s, z_r, x_s, x_r, y_s, y_r,
                    load_sem, x_sem, xs_s, xs_r, turn_s, turn_r, out_s, out_r):
    dp = lax.axis_index("dp")
    tp = lax.axis_index("tp")
    y = dp // 4
    zh = dp % 4
    x = tp // 4
    zl = tp // 2 % 2
    c = tp % 2
    rows, length = z_in.shape[1:]
    cols = xs.shape[3]
    sibling = (dp, x * 4 + zl * 2 + (1 - c))
    across = (dp, x * 4 + (1 - zl) * 2 + c)
    around = [(lax.rem(y + j, 4) * 4 + zh, tp) for j in range(4)]
    beside = [(dp, lax.rem(x + j, 4) * 4 + zl * 2 + c) for j in range(4)]

    barrier = pltpu.get_barrier_semaphore()
    for partner in (sibling, across, *beside[1:], *around[1:]):
        pl.semaphore_signal(barrier, 1, device_id=partner, device_id_type=MESH)

    def dest(u, h):
        return y * 4 + h, x * 4 + c * 2 + u

    def is_other(d, t):
        return jnp.logical_or(d != dp, t != tp)

    def greet(d, t, n):
        other = is_other(d, t)

        @pl.when(other)
        def _():
            pl.semaphore_signal(barrier, 1, device_id=(d, t), device_id_type=MESH)
        return n + jnp.where(other, 1, 0)

    n = lax.fori_loop(0, 8, lambda i, n: greet(*dest(i % 2, i // 2), n), jnp.int32(8))
    n = lax.fori_loop(0, 8, lambda i, n: greet(y * 4 + i // 2, x * 4 + i % 2 * 2 + zl, n), n)

    load = pltpu.make_async_copy(kvt.at[c], own, load_sem)
    load.start()
    x_loads = []
    for j, src in enumerate((x_own, x1, x2, x3)):
        cp = pltpu.make_async_copy(src, xs.at[lax.rem(x + 4 - j, 4), c], x_sem.at[j])
        cp.start()
        x_loads.append(cp)

    pl.semaphore_wait(barrier, n)

    started = []

    def send(src, dst, ss, rs, to):
        cp = pltpu.make_async_remote_copy(src_ref=src, dst_ref=dst, send_sem=ss, recv_sem=rs,
                                          device_id=to, device_id_type=MESH)
        cp.start()
        started.append(cp)
        return cp

    def cut(k):
        return pl.ds(k * rows, rows)

    core = [send(kvt.at[1 - c, :, cut(k)], core_in.at[k], core_s.at[k], core_r.at[k], sibling)
            for k in range(CHUNKS)]
    load.wait()

    zc, hc, yc, tc, xc = ([] for _ in range(5))

    def share(j):
        x_loads[j].wait()
        here = xs.at[lax.rem(x + 4 - j, 4), c]
        xc.append(send(here, here, xs_s.at[j], xs_r.at[j], sibling))

    def reduce_core(k):
        core[k].wait_recv()
        part[k] = (own[1 - zl, cut(k)].astype(F32) + core_in[k, 1 - zl].astype(F32)).astype(BF16)
        zc.append(send(part.at[k], z_in.at[k], z_s.at[k], z_r.at[k], across))

    def reduce_z(k):
        zc[k].wait_recv()
        heads[k, x] = (own[zl, cut(k)].astype(F32) + core_in[k, zl].astype(F32) + z_in[k].astype(F32)).astype(BF16)
        here = heads.at[k, x]
        hc.append([send(here, here, x_s.at[k, j - 1], x_r.at[k, j - 1], beside[j]) for j in (2, 1, 3)])

    def multiply(k):
        for cp in hc[k]:
            cp.wait_recv()
        if k == 0:
            for cp in xc:
                cp.wait_recv()
        lhs = heads[k].reshape(4 * rows, length)
        res = jnp.dot(lhs, xs[...].reshape(length, cols), preferred_element_type=F32)
        wide = cols // 4
        for q in range(4):
            prod[k, q] = res[:, q * wide:(q + 1) * wide]
        sent = []
        for j in (2, 1, 3):
            y_out[k, j - 1] = prod[k, lax.rem(y + j, 4)].astype(BF16)
            sent.append(send(y_out.at[k, j - 1], y_in.at[k, j - 1], y_s.at[k, j - 1], y_r.at[k, j - 1], around[j]))
        yc.append(sent)

    spot = zh * 2 + zl

    def out_copy(k, q):
        d, t = dest(k // PARTS, lax.rem(x + 4 - q, 4))
        return d, t, pltpu.make_async_remote_copy(
            src_ref=turned.at[k, q], dst_ref=landed.at[spot, k % PARTS], send_sem=out_s.at[k * 4 + q],
            recv_sem=out_r.at[spot, k % PARTS], device_id=(d, t), device_id_type=MESH)

    def deliver(k):
        for cp in yc[k]:
            cp.wait_recv()
        total = (prod[k, y] + y_in[k, 0].astype(F32) + y_in[k, 1].astype(F32) + y_in[k, 2].astype(F32)).astype(BF16)
        for h in range(4):
            final[k, h] = total[h * rows:(h + 1) * rows]
        turned[k, 0] = final[k, x]
        tc.append([send(final.at[k, lax.rem(x + j, 4)], turned.at[k, j], turn_s.at[k, j - 1], turn_r.at[k, j - 1],
                        beside[j]) for j in (2, 1, 3)])

    def scatter(k):
        for cp in tc[k]:
            cp.wait_recv()

        def one(q, carry):
            d, t, cp = out_copy(k, q)
            other = is_other(d, t)

            @pl.when(other)
            def _():
                cp.start()

            @pl.when(jnp.logical_not(other))
            def _():
                pltpu.make_async_copy(turned.at[k, q], landed.at[spot, k % PARTS], out_r.at[spot, k % PARTS]).start()
            return carry
        lax.fori_loop(0, 4, one, 0)

    stages = (reduce_core, reduce_z, multiply, deliver, scatter)
    order = sorted((start + k * gap, i, k) for i, (start, gap) in enumerate(TIMES) for k in range(CHUNKS))
    order = sorted(order + [(SHARE[j], -1, j) for j in range(4)])
    for _, i, k in order:
        share(k) if i < 0 else stages[i](k)

    def collect(i, total):
        new = []
        for p in range(PARTS):
            pltpu.make_async_copy(landed.at[i, p], landed.at[i, p], out_r.at[i, p]).wait()
            new.append(total[p] + landed[i, p].astype(F32))
        return tuple(new)

    zero = jnp.zeros((rows, cols // 4), F32)
    sums = lax.fori_loop(0, 8, collect, (zero,) * PARTS)
    for p in range(PARTS):
        out_ref[p * rows:(p + 1) * rows] = sums[p]

    for cp in started:
        cp.wait_send()

    def drain(j, carry):
        d, t, cp = out_copy(j // 4, j % 4)

        @pl.when(is_other(d, t))
        def _():
            cp.wait_send()
        return carry
    lax.fori_loop(0, 4 * CHUNKS, drain, 0)


def exchange(kvt, x_own, others):
    length = kvt.shape[3]
    cols = x_own.shape[1]
    rows = HD // CHUNKS
    sem = pltpu.SemaphoreType.DMA
    n = CHUNKS
    return pl.pallas_call(
        exchange_kernel,
        out_shape=jax.ShapeDtypeStruct((PARTS * rows, cols // 4), F32),
        in_specs=[pl.BlockSpec(memory_space=pl.ANY)] * 5,
        out_specs=pl.BlockSpec(memory_space=pltpu.VMEM),
        scratch_shapes=[
            pltpu.VMEM((2, HD, length), BF16), pltpu.VMEM((n, 2, rows, length), BF16),
            pltpu.VMEM((n, rows, length), BF16), pltpu.VMEM((n, rows, length), BF16),
            pltpu.VMEM((n, 4, rows, length), BF16), pltpu.VMEM((4, 2, TILE, cols), BF16),
            pltpu.VMEM((n, 4, 4 * rows, cols // 4), F32),
            pltpu.VMEM((n, 3, 4 * rows, cols // 4), BF16), pltpu.VMEM((n, 3, 4 * rows, cols // 4), BF16),
            pltpu.VMEM((n, 4, rows, cols // 4), BF16), pltpu.VMEM((n, 4, rows, cols // 4), BF16),
            pltpu.VMEM((8, PARTS, rows, cols // 4), BF16),
        ] + [sem((n,))] * 4 + [sem((n, 3))] * 4 + [sem, sem((4,)), sem((4,)), sem((4,)),
                                                    sem((n, 3)), sem((n, 3)), sem((4 * n,)), sem((8, PARTS))],
        compiler_params=pltpu.CompilerParams(collective_id=0, has_side_effects=True, vmem_limit_bytes=40 << 20),
        cost_estimate=pl.CostEstimate(flops=10**9, bytes_accessed=8 << 20, transcendentals=0),
        name="exchange",
    )(kvt, x_own, *others)


def deal_kernel(x_in, *outs):
    x = lax.axis_index("tp") // 4
    wide = outs[0].shape[1] // 4
    for j in range(4):
        for i in range(4):
            cols = pl.ds(pl.multiple_of((4 * i + lax.rem(x + j, 4)) * wide, wide), wide)
            outs[j][:, i * wide:(i + 1) * wide] = x_in[:, cols]


def deal(rows):
    vmem = pl.BlockSpec(memory_space=pltpu.VMEM)
    shape = jax.ShapeDtypeStruct((rows.shape[0], rows.shape[1] // 4), BF16)
    return pl.pallas_call(deal_kernel, out_shape=[shape] * 4, in_specs=[vmem], out_specs=[vmem] * 4, name="deal")(rows)


def local(input_rows, queries, key_values, out_grad, item_logratio, pair_ids, tile_item, tile_image):
    rows = input_rows[0]
    others = []
    mine, *blocks = deal(rows)
    for dx, block in zip(range(1, 4), blocks):
        others.append(lax.ppermute(block, "tp", [(a, (a + 4 * dx) % 16) for a in range(16)]))
    dq, kvt = attention(queries, out_grad, key_values, item_logratio, pair_ids, tile_item, tile_image)
    return dq, exchange(kvt, mine, others).T


def solution(mesh):
    in_specs = (P("dp", "tp", None), P("dp", None, "tp"), P("dp", None, None), P("dp", None, "tp"),
                P("dp", None), P("dp", None), P("dp", None), P("dp", None))
    out_specs = (P("dp", None, "tp"), P("dp", "tp"))
    return jax.shard_map(local, mesh=mesh, in_specs=in_specs, out_specs=out_specs, check_vma=False)
```

```python
import functools, math
import jax, jax.numpy as jnp
from jax import lax
from jax.experimental import pallas as pl
from jax.experimental.pallas import tpu as pltpu

from jax.sharding import PartitionSpec as P

KVH = 4; HD = 128; TILE = 128; BETA = 0.1
MASKED = -1e30
LOG2E = 1.4426950408889634

def attention_kernel(ratio_h, pair_h, item_h, image_h, q_hbm, og_hbm, kv_hbm, dq_hbm, kvt_hbm,
                     kvt_ref, kv, q_ref, og_ref, dq_ref, s0, s1, dp0, dp1, acc, ratio, pair, item, image,
                     lo_s, hi_s, n_s, spot, order, work, z_s, small_sem, big_sem, dq_sem, kvt_sem):
    group = lax.axis_size("tp") // KVH
    g = lax.axis_index("tp") // group
    nt = item.shape[1]
    items = ratio.shape[1]
    small = [pltpu.make_async_copy(a, b, small_sem.at[i])
             for i, (a, b) in enumerate(((ratio_h, ratio), (pair_h, pair), (item_h, item), (image_h, image)))]
    for cp in small:
        cp.start()
    big = [pltpu.make_async_copy(kv_hbm.at[0, :, pl.ds(pl.multiple_of(g * 2 * HD, 2 * HD), 2 * HD)], kv, big_sem.at[0]),
           pltpu.make_async_copy(q_hbm.at[0], q_ref, big_sem.at[1]),
           pltpu.make_async_copy(og_hbm.at[0], og_ref, big_sem.at[2])]
    for cp in big:
        cp.start()
    inv_root = 1.0 / math.sqrt(HD)
    c2 = inv_root * LOG2E
    W = 2 * TILE
    acc[...] = jnp.zeros_like(acc)
    for cp in small:
        cp.wait()
    lo_s[0] = 0
    for i in range(1, nt):
        lo_s[i] = jnp.where(item[0, i] == item[0, i - 1], lo_s[i - 1], i)
    hi_s[nt - 1] = nt - 1
    for i in reversed(range(nt - 1)):
        same = (image[0, i] > 0) & (image[0, i] == image[0, i + 1]) & (item[0, i] == item[0, i + 1])
        hi_s[i] = jnp.where(same, hi_s[i + 1], i)
    for a in range(items):
        other = jnp.float32(0.0)
        p = jnp.float32(1.0)
        for b in range(items):
            if b != a:
                same = pair[0, a] == pair[0, b]
                other = other + jnp.where(same, ratio[0, b], 0.0)
                if a < b:
                    p = jnp.where(same, -1.0, p)
        z_s[a] = BETA * p * (other - ratio[0, a])
        z_s[items + a] = p

    for i in range(nt):
        n_s[i] = (hi_s[i] - lo_s[i] + 2) // 2

    for n in range(nt // 2 + 1):
        spot[n] = 0
    for i in range(nt):
        spot[n_s[i]] = spot[n_s[i]] + 1
    start = jnp.int32(0)
    for n in reversed(range(1, nt // 2 + 1)):
        here = spot[n]
        spot[n] = start
        start = start + here
    for i in range(nt):
        order[spot[n_s[i]]] = i
        spot[n_s[i]] = spot[n_s[i]] + 1

    def match(t, carry):
        i, w = carry
        a = order[jnp.minimum(i, nt - 1)]
        b = order[jnp.minimum(i + 1, nt - 1)]
        both = (i + 1 < nt) & (n_s[a] - n_s[b] <= 1)
        more = i < nt
        work[3 * w] = a
        work[3 * w + 1] = jnp.where(both, b, a)
        work[3 * w + 2] = jnp.where(both, 1, 0)
        return i + jnp.where(both, 2, 1), w + jnp.where(more, 1, 0)

    _, count = lax.fori_loop(0, nt, match, (jnp.int32(0), jnp.int32(0)))
    for cp in big:
        cp.wait()

    def block(I, real, n, spare, s_scr, dp_scr):
        lo = lo_s[I]
        hi = hi_s[I]
        img = image[0, I]
        it = item[0, I]
        r0 = pl.multiple_of(I * TILE, TILE)
        st = pl.multiple_of(jnp.clip(hi + 1 - 2 * n, 0, nt - 2 * n) * TILE, TILE)
        first = lo * TILE - st
        v = {}

        def stage1():
            qi = q_ref[pl.ds(r0, TILE), :]
            q2 = jnp.concatenate([qi[:, :HD], qi[:, HD:]], axis=0)
            coef = z_s[items + it] * real.astype(jnp.float32) / (1.0 + jnp.exp(jnp.full((8, HD), z_s[it], jnp.float32)))
            coef = jnp.concatenate([coef[:1], coef[:1]], axis=1)
            wi = (og_ref[pl.ds(r0, TILE), :].astype(jnp.float32) * coef).astype(jnp.bfloat16)
            w2 = jnp.concatenate([wi[:, :HD], wi[:, HD:]], axis=0)
            v["q2t"] = q2.T
            v["w2t"] = w2.T
            row = lax.broadcasted_iota(jnp.int32, (TILE, 1), 0)
            row = jnp.concatenate([row, row], axis=0)
            last = jnp.where(img > 0, jnp.full((2 * TILE, 1), (hi + 1) * TILE - 1 - st), r0 - st + row)
            m = None
            for ch in range(n):
                rows = pl.ds(st + ch * W, W)
                s = lax.dot_general(q2, kv[rows, :HD], (((1,), (1,)), ((), ())), preferred_element_type=jnp.float32)
                if ch <= spare or ch >= n - 2:
                    col = lax.broadcasted_iota(jnp.int32, (1, W), 1) + ch * W
                    s = jnp.where(jnp.where(col >= first, col, nt * TILE) <= last, s, MASKED)
                s_scr[:, ch * W:(ch + 1) * W] = s
                mm = jnp.maximum(s[:, :HD], s[:, HD:])
                m = mm if m is None else jnp.maximum(m, mm)
                dp_scr[:, ch * W:(ch + 1) * W] = lax.dot_general(
                    w2, kv[rows, HD:], (((1,), (1,)), ((), ())), preferred_element_type=jnp.float32)
            v["m"] = jnp.max(m, axis=1, keepdims=True) * c2

        def stage2():
            mr = v["m"]
            l = r = None
            for ch in range(n):
                cols = slice(ch * W, (ch + 1) * W)
                p = jnp.exp2(s_scr[:, cols] * c2 - mr)
                s_scr[:, cols] = p
                pd = p * dp_scr[:, cols]
                ll = p[:, :HD] + p[:, HD:]
                rr = pd[:, :HD] + pd[:, HD:]
                l = ll if l is None else l + ll
                r = rr if r is None else r + rr
            v["inv"] = 1.0 / jnp.sum(l, axis=1, keepdims=True)
            v["rd"] = jnp.sum(r, axis=1, keepdims=True) * v["inv"]

        def stage3():
            inv, rd = v["inv"], v["rd"]
            dq = None
            for ch in range(n):
                rows = pl.ds(st + ch * W, W)
                cols = slice(ch * W, (ch + 1) * W)
                at = s_scr[:, cols] * inv
                ds = (at * (dp_scr[:, cols] - rd)).astype(jnp.bfloat16)
                at = at.astype(jnp.bfloat16)
                d = jnp.dot(ds, kv[rows, :HD], preferred_element_type=jnp.float32)
                dq = d if dq is None else dq + d
                acc[:HD, rows] += jnp.dot(v["q2t"], ds, preferred_element_type=jnp.float32)
                acc[HD:, rows] += jnp.dot(v["w2t"], at, preferred_element_type=jnp.float32)
            dq = (dq * inv_root).astype(jnp.bfloat16)
            to = pl.ds(pl.multiple_of(jnp.where(real > 0, I, nt) * TILE, TILE), TILE)
            dq_ref[to, :HD] = dq[:TILE]
            dq_ref[to, HD:] = dq[TILE:]

        return stage1, stage2, stage3

    def out_copy(i):
        here = pl.ds(pl.multiple_of(i * TILE, TILE), TILE)
        return pltpu.make_async_copy(dq_ref.at[here], dq_hbm.at[0, here], dq_sem.at[i])

    def row_pair(j, carry):
        a, b, real = work[3 * j], work[3 * j + 1], work[3 * j + 2]
        n_here = n_s[a]
        for n in range(1, nt // 2 + 1):
            @pl.when(n_here == n)
            def _():
                one = block(a, jnp.int32(1), n, 1, s0, dp0)
                two = block(b, real, n, 1, s1, dp1)
                for f, g2 in zip(one, two):
                    f()
                    g2()
        out_copy(a).start()

        @pl.when(real > 0)
        def _():
            out_copy(b).start()
        return carry

    lax.fori_loop(0, count, row_pair, 0)
    kvt_out = []
    for part in range(2):
        for z in range(2):
            for i in range(nt // 4):
                frm = slice((2 * i + z) * W, (2 * i + z + 1) * W)
                block = acc[part * HD:(part + 1) * HD, frm]
                kvt_ref[part, z, :, i * W:(i + 1) * W] = (block if part else block * inv_root).astype(jnp.bfloat16)
            cp = pltpu.make_async_copy(kvt_ref.at[part, z], kvt_hbm.at[part, z], kvt_sem.at[part, z])
            cp.start()
            kvt_out.append(cp)

    def finish(i, carry):
        out_copy(i).wait()
        return carry
    lax.fori_loop(0, nt, finish, 0)
    for cp in kvt_out:
        cp.wait()


def attention(queries, out_grad, key_values, ratio, pair, item, image):
    L = queries.shape[1]
    nt = L // TILE
    hbm = pl.BlockSpec(memory_space=pl.ANY)
    wide = pltpu.VMEM((2 * TILE, L), jnp.float32)
    low = pltpu.VMEM((L, 2 * HD), jnp.bfloat16)
    return pl.pallas_call(
        attention_kernel,
        out_shape=[jax.ShapeDtypeStruct(queries.shape, jnp.bfloat16),
                   jax.ShapeDtypeStruct((2, 2, HD, L // 2), jnp.bfloat16)],
        in_specs=[hbm] * 7,
        out_specs=[hbm, hbm],
        scratch_shapes=[pltpu.VMEM((2, 2, HD, L // 2), jnp.bfloat16), low, low, low, pltpu.VMEM((L + TILE, 2 * HD), jnp.bfloat16), wide, wide, wide, wide,
            pltpu.VMEM((2 * HD, L), jnp.float32),
            pltpu.SMEM(ratio.shape, jnp.float32),
            pltpu.SMEM(pair.shape, jnp.int32),
            pltpu.SMEM(item.shape, jnp.int32),
            pltpu.SMEM(image.shape, jnp.int32),
            pltpu.SMEM((nt,), jnp.int32),
            pltpu.SMEM((nt,), jnp.int32),
            pltpu.SMEM((nt,), jnp.int32),
            pltpu.SMEM((nt // 2 + 1,), jnp.int32),
            pltpu.SMEM((nt + 1,), jnp.int32),
            pltpu.SMEM((3 * (nt + 1),), jnp.int32),
            pltpu.SMEM((2 * ratio.shape[1],), jnp.float32),
            pltpu.SemaphoreType.DMA((4,)), pltpu.SemaphoreType.DMA((3,)), pltpu.SemaphoreType.DMA((nt,)), pltpu.SemaphoreType.DMA((2, 2)),
        ],
        compiler_params=pltpu.CompilerParams(vmem_limit_bytes=56 << 20),
        cost_estimate=pl.CostEstimate(flops=10 * 10**9, bytes_accessed=8 << 20, transcendentals=0),
        name="attention",
    )(ratio, pair, item, image, queries, out_grad, key_values)


CHUNKS = 4
PARTS = CHUNKS // 2
TIMES = ((0, 1), (1, 1), (3.2, 1), (5.4, 1), (7.5, 1))
SHARE = (0.5, 0.5, 0.5, 0.5)
MESH = pl.DeviceIdType.MESH
F32 = jnp.float32
BF16 = jnp.bfloat16


def exchange_kernel(kvt, x_own, x1, x2, x3, out_ref,
                    own, core_in, part, z_in, heads, xs, prod, y_out, y_in, final, turned, landed,
                    core_s, core_r, z_s, z_r, x_s, x_r, y_s, y_r,
                    load_sem, x_sem, xs_s, xs_r, turn_s, turn_r, out_s, out_r):
    dp = lax.axis_index("dp")
    tp = lax.axis_index("tp")
    y = dp // 4
    zh = dp % 4
    x = tp // 4
    zl = tp // 2 % 2
    c = tp % 2
    rows, length = z_in.shape[1:]
    cols = xs.shape[3]
    sibling = (dp, x * 4 + zl * 2 + (1 - c))
    across = (dp, x * 4 + (1 - zl) * 2 + c)
    around = [(lax.rem(y + j, 4) * 4 + zh, tp) for j in range(4)]
    beside = [(dp, lax.rem(x + j, 4) * 4 + zl * 2 + c) for j in range(4)]

    barrier = pltpu.get_barrier_semaphore()
    for partner in (sibling, across, *beside[1:], *around[1:]):
        pl.semaphore_signal(barrier, 1, device_id=partner, device_id_type=MESH)

    def dest(u, h):
        return y * 4 + h, x * 4 + c * 2 + u

    def is_other(d, t):
        return jnp.logical_or(d != dp, t != tp)

    def greet(d, t, n):
        other = is_other(d, t)

        @pl.when(other)
        def _():
            pl.semaphore_signal(barrier, 1, device_id=(d, t), device_id_type=MESH)
        return n + jnp.where(other, 1, 0)

    n = lax.fori_loop(0, 8, lambda i, n: greet(*dest(i % 2, i // 2), n), jnp.int32(8))
    n = lax.fori_loop(0, 8, lambda i, n: greet(y * 4 + i // 2, x * 4 + i % 2 * 2 + zl, n), n)

    load = pltpu.make_async_copy(kvt.at[c], own, load_sem)
    load.start()
    x_loads = []
    for j, src in enumerate((x_own, x1, x2, x3)):
        cp = pltpu.make_async_copy(src, xs.at[lax.rem(x + 4 - j, 4), c], x_sem.at[j])
        cp.start()
        x_loads.append(cp)

    pl.semaphore_wait(barrier, n)

    started = []

    def send(src, dst, ss, rs, to):
        cp = pltpu.make_async_remote_copy(src_ref=src, dst_ref=dst, send_sem=ss, recv_sem=rs,
                                          device_id=to, device_id_type=MESH)
        cp.start()
        started.append(cp)
        return cp

    def cut(k):
        return pl.ds(k * rows, rows)

    core = [send(kvt.at[1 - c, :, cut(k)], core_in.at[k], core_s.at[k], core_r.at[k], sibling)
            for k in range(CHUNKS)]
    load.wait()

    zc, hc, yc, tc, xc = ([] for _ in range(5))

    def share(j):
        x_loads[j].wait()
        here = xs.at[lax.rem(x + 4 - j, 4), c]
        xc.append(send(here, here, xs_s.at[j], xs_r.at[j], sibling))

    def reduce_core(k):
        core[k].wait_recv()
        part[k] = (own[1 - zl, cut(k)].astype(F32) + core_in[k, 1 - zl].astype(F32)).astype(BF16)
        zc.append(send(part.at[k], z_in.at[k], z_s.at[k], z_r.at[k], across))

    def reduce_z(k):
        zc[k].wait_recv()
        heads[k, x] = (own[zl, cut(k)].astype(F32) + core_in[k, zl].astype(F32) + z_in[k].astype(F32)).astype(BF16)
        here = heads.at[k, x]
        hc.append([send(here, here, x_s.at[k, j - 1], x_r.at[k, j - 1], beside[j]) for j in (2, 1, 3)])

    def multiply(k):
        for cp in hc[k]:
            cp.wait_recv()
        if k == 0:
            for cp in xc:
                cp.wait_recv()
        lhs = heads[k].reshape(4 * rows, length)
        res = jnp.dot(lhs, xs[...].reshape(length, cols), preferred_element_type=F32)
        wide = cols // 4
        for q in range(4):
            prod[k, q] = res[:, q * wide:(q + 1) * wide]
        sent = []
        for j in (2, 1, 3):
            y_out[k, j - 1] = prod[k, lax.rem(y + j, 4)].astype(BF16)
            sent.append(send(y_out.at[k, j - 1], y_in.at[k, j - 1], y_s.at[k, j - 1], y_r.at[k, j - 1], around[j]))
        yc.append(sent)

    spot = zh * 2 + zl

    def out_copy(k, q):
        d, t = dest(k // PARTS, lax.rem(x + 4 - q, 4))
        return d, t, pltpu.make_async_remote_copy(
            src_ref=turned.at[k, q], dst_ref=landed.at[spot, k % PARTS], send_sem=out_s.at[k * 4 + q],
            recv_sem=out_r.at[spot, k % PARTS], device_id=(d, t), device_id_type=MESH)

    def deliver(k):
        for cp in yc[k]:
            cp.wait_recv()
        total = (prod[k, y] + y_in[k, 0].astype(F32) + y_in[k, 1].astype(F32) + y_in[k, 2].astype(F32)).astype(BF16)
        for h in range(4):
            final[k, h] = total[h * rows:(h + 1) * rows]
        turned[k, 0] = final[k, x]
        tc.append([send(final.at[k, lax.rem(x + j, 4)], turned.at[k, j], turn_s.at[k, j - 1], turn_r.at[k, j - 1],
                        beside[j]) for j in (2, 1, 3)])

    def scatter(k):
        for cp in tc[k]:
            cp.wait_recv()

        def one(q, carry):
            d, t, cp = out_copy(k, q)
            other = is_other(d, t)

            @pl.when(other)
            def _():
                cp.start()

            @pl.when(jnp.logical_not(other))
            def _():
                pltpu.make_async_copy(turned.at[k, q], landed.at[spot, k % PARTS], out_r.at[spot, k % PARTS]).start()
            return carry
        lax.fori_loop(0, 4, one, 0)

    stages = (reduce_core, reduce_z, multiply, deliver, scatter)
    order = sorted((start + k * gap, i, k) for i, (start, gap) in enumerate(TIMES) for k in range(CHUNKS))
    order = sorted(order + [(SHARE[j], -1, j) for j in range(4)])
    for _, i, k in order:
        share(k) if i < 0 else stages[i](k)

    def collect(i, total):
        new = []
        for p in range(PARTS):
            pltpu.make_async_copy(landed.at[i, p], landed.at[i, p], out_r.at[i, p]).wait()
            new.append(total[p] + landed[i, p].astype(F32))
        return tuple(new)

    zero = jnp.zeros((rows, cols // 4), F32)
    sums = lax.fori_loop(0, 8, collect, (zero,) * PARTS)
    for p in range(PARTS):
        out_ref[p * rows:(p + 1) * rows] = sums[p]

    for cp in started:
        cp.wait_send()

    def drain(j, carry):
        d, t, cp = out_copy(j // 4, j % 4)

        @pl.when(is_other(d, t))
        def _():
            cp.wait_send()
        return carry
    lax.fori_loop(0, 4 * CHUNKS, drain, 0)


def exchange(kvt, x_own, others):
    length = kvt.shape[3]
    cols = x_own.shape[1]
    rows = HD // CHUNKS
    sem = pltpu.SemaphoreType.DMA
    n = CHUNKS
    return pl.pallas_call(
        exchange_kernel,
        out_shape=jax.ShapeDtypeStruct((PARTS * rows, cols // 4), F32),
        in_specs=[pl.BlockSpec(memory_space=pl.ANY)] * 5,
        out_specs=pl.BlockSpec(memory_space=pltpu.VMEM),
        scratch_shapes=[
            pltpu.VMEM((2, HD, length), BF16), pltpu.VMEM((n, 2, rows, length), BF16),
            pltpu.VMEM((n, rows, length), BF16), pltpu.VMEM((n, rows, length), BF16),
            pltpu.VMEM((n, 4, rows, length), BF16), pltpu.VMEM((4, 2, TILE, cols), BF16),
            pltpu.VMEM((n, 4, 4 * rows, cols // 4), F32),
            pltpu.VMEM((n, 3, 4 * rows, cols // 4), BF16), pltpu.VMEM((n, 3, 4 * rows, cols // 4), BF16),
            pltpu.VMEM((n, 4, rows, cols // 4), BF16), pltpu.VMEM((n, 4, rows, cols // 4), BF16),
            pltpu.VMEM((8, PARTS, rows, cols // 4), BF16),
        ] + [sem((n,))] * 4 + [sem((n, 3))] * 4 + [sem, sem((4,)), sem((4,)), sem((4,)),
                                                    sem((n, 3)), sem((n, 3)), sem((4 * n,)), sem((8, PARTS))],
        compiler_params=pltpu.CompilerParams(collective_id=0, has_side_effects=True, vmem_limit_bytes=40 << 20),
        cost_estimate=pl.CostEstimate(flops=10**9, bytes_accessed=8 << 20, transcendentals=0),
        name="exchange",
    )(kvt, x_own, *others)


def deal_kernel(x_in, *outs):
    x = lax.axis_index("tp") // 4
    wide = outs[0].shape[1]
    for j in range(4):
        outs[j][...] = x_in[:, pl.ds(pl.multiple_of(lax.rem(x + j, 4) * wide, wide), wide)]


def deal(rows):
    high, cols = rows.shape[0], rows.shape[1] // 4
    shape = jax.ShapeDtypeStruct((high, cols), BF16)
    return pl.pallas_call(
        deal_kernel, out_shape=[shape] * 4, grid=(4,), name="deal",
        in_specs=[pl.BlockSpec((high, cols), lambda i: (0, i))],
        out_specs=[pl.BlockSpec((high, cols // 4), lambda i: (0, i))] * 4,
    )(rows)


def local(input_rows, queries, key_values, out_grad, item_logratio, pair_ids, tile_item, tile_image):
    rows = input_rows[0]
    others = []
    mine, *blocks = deal(rows)
    for dx, block in zip(range(1, 4), blocks):
        others.append(lax.ppermute(block, "tp", [(a, (a + 4 * dx) % 16) for a in range(16)]))
    dq, kvt = attention(queries, out_grad, key_values, item_logratio, pair_ids, tile_item, tile_image)
    return dq, exchange(kvt, mine, others).T


def solution(mesh):
    in_specs = (P("dp", "tp", None), P("dp", None, "tp"), P("dp", None, None), P("dp", None, "tp"),
                P("dp", None), P("dp", None), P("dp", None), P("dp", None))
    out_specs = (P("dp", None, "tp"), P("dp", "tp"))
    return jax.shard_map(local, mesh=mesh, in_specs=in_specs, out_specs=out_specs, check_vma=False)
```
